32 devices in a mesh: seg: 4 (over y, x), blk: 8 (over z, core).
Axes of the slice: x: 2, y: 2, z: 4, core: 2. Of those that a mesh axis runs over, the one named last changes fastest.
Arguments:
- guess_a: bfloat16 [4, 8, 2, 256, 256], P('seg', 'blk'), may hold values from -6 to 6
- guess_b: bfloat16 [4, 8, 2, 256, 256], P('seg', 'blk'), may hold values from -6 to 6
- left_env_a: bfloat16 [4, 12, 8, 2, 256, 256], P('seg', None, 'blk')
- right_env_a: bfloat16 [4, 12, 8, 2, 256, 256], P('seg', None, 'blk')
- left_env_b: bfloat16 [4, 12, 8, 2, 256, 256], P('seg', None, 'blk')
- right_env_b: bfloat16 [4, 12, 8, 2, 256, 256], P('seg', None, 'blk')
- channel_mix: float32 [12, 12], replicated, may hold values from -1.75 to 1.75
- term_shift: int32 [12], replicated, may hold values from 0 to 4, as said below
- sector_sizes: int32 [4, 4, 8, 2], P('seg', None, 'blk'), may hold values from 32 to 256, as said below
- edge_state: bfloat16 [8, 2, 256, 256], P('blk'), may hold values from -6 to 6
Outputs:
- ground_a: float32 [4, 8, 2, 256, 256], P('seg', 'blk')
- ground_b: float32 [4, 8, 2, 256, 256], P('seg', 'blk')
- energies: float32 [4, 2], P('seg')
- boundary_env: bfloat16 [4, 12, 8, 2, 256, 256], P('seg', None, 'blk')
The draws below stay inside these ranges and needn't reach their ends.
Inputs may be any that keep to these rules, and one draw needn't show every extreme that they name: `sector_sizes`: each of the four tables of every segment reaches 256 and 32. `term_shift`: every code 0 to 4 appears at least once.
All inputs are finite; a program needn't handle non-finite values.
Results may differ from the reference program's by a relative error of at most 0.0088.
Values may be sent and summed in bfloat16 or wider, within the bound.
No kernel may reach another device: no remote copies, remote signals or barrier semaphores. Data moves between devices by JAX's collectives and lax.ppermute only.
A program may use at most 128 MiB of HBM per device.

```python
import jax
import jax.numpy as jnp
from jax import lax

ND = 2
BS = 256
W = 12
NSEG = 4
NU = 8


def draw_sector_sizes(key, part):
    key = jax.random.fold_in(key, 11)
    places = jnp.arange(NU, dtype=jnp.int32)
    center = NU // 2
    slope = BS // 2 // max(NU // 2, 1)
    base_rows = BS - jnp.abs(places - center) * slope
    jitter = jax.random.randint(key, (NSEG, 4, NU, ND), 0, max(BS // 8, 1), dtype=jnp.int32)
    sizes = jnp.clip(base_rows[None, None, :, None] - jitter, BS // 8, BS)
    sizes = sizes.at[:, :, center, 0].set(BS)
    sizes = sizes.at[:, :, 0, 1].set(BS // 8)
    return sizes.astype(jnp.int32)


def draw_term_shift(key, part):
    key = jax.random.fold_in(key, 12)
    head_key, tail_key = jax.random.split(key)
    leading = jax.random.permutation(head_key, jnp.arange(5, dtype=jnp.int32))
    trailing = jax.random.randint(tail_key, (W - 5,), 0, 5, dtype=jnp.int32)
    return jnp.concatenate([leading, trailing]).astype(jnp.int32)


def environment_blocks(key, top_rise):
    shape = (NSEG, W, NU, ND, BS, BS)
    noise_key, scale_key = jax.random.split(key)
    noise = jax.random.normal(noise_key, shape, jnp.float32)
    noise = noise * BS ** (-0.5)
    places = jnp.arange(NU, dtype=jnp.float32) / (NU - 1)
    rise = 0.5 * jnp.exp(places * jnp.log(top_rise / 0.5))
    jitter = jax.random.uniform(scale_key, (NSEG, 1, NU, ND, 1, 1), jnp.float32, 0.85, 1.15)
    scale = jnp.sqrt(rise / W)[None, None, :, None, None, None] * jitter
    identity = jnp.eye(BS, dtype=jnp.float32)
    return (scale * (identity + noise)).astype(jnp.bfloat16)


def draw_left_env_a(key, part):
    key = jax.random.fold_in(key, 21)
    return environment_blocks(key, 4.0)


def draw_right_env_a(key, part):
    key = jax.random.fold_in(key, 22)
    return environment_blocks(key, 4.0)


def draw_left_env_b(key, part):
    key = jax.random.fold_in(key, 23)
    return environment_blocks(key, 4.0)


def draw_right_env_b(key, part):
    key = jax.random.fold_in(key, 24)
    return environment_blocks(key, 4.0)


def level_of(rng, shape, shards, low, top_value):
    gain = 1.0
    for position, shards_of in shards:
        heights = jax.random.uniform(jax.random.fold_in(jax.random.fold_in(rng, 6), position), (shards_of,), jnp.float32, low / len(shards), top_value / len(shards))
        gain = gain * jnp.repeat(jnp.exp(heights), shape[position] // shards_of).reshape((-1,) + (1,) * (len(shape) - 1 - position))
    return gain


def gaussian(rng, extent, width, limit, pieces=(), kind=jnp.bfloat16):
    gain = level_of(rng, extent, pieces, -0.22, 0.18) if pieces else 1.0
    values = jax.random.normal(rng, extent, jnp.float32) * width * gain
    return jnp.minimum(jnp.maximum(values, -limit), limit).astype(kind)


def setup_inputs(seed: int = 0) -> dict:
    key_list = jax.random.split(jax.random.key(seed), 11)
    return {
        "guess_a": gaussian(key_list[0], (NSEG, NU, ND, BS, BS), 1.0, 6.0, ((0, 4), (1, 8))),
        "guess_b": gaussian(key_list[1], (NSEG, NU, ND, BS, BS), 1.0, 6.0, ((0, 4), (1, 8))),
        "left_env_a": draw_left_env_a(jax.random.fold_in(key_list[10], 71), 0),
        "right_env_a": draw_right_env_a(jax.random.fold_in(key_list[10], 71), 0),
        "left_env_b": draw_left_env_b(jax.random.fold_in(key_list[10], 71), 0),
        "right_env_b": draw_right_env_b(jax.random.fold_in(key_list[10], 71), 0),
        "channel_mix": gaussian(key_list[6], (W, W), W ** -0.5, 1.75, (), jnp.float32),
        "term_shift": draw_term_shift(jax.random.fold_in(key_list[10], 71), 0),
        "sector_sizes": draw_sector_sizes(jax.random.fold_in(key_list[10], 71), 0),
        "edge_state": gaussian(key_list[9], (NU, ND, BS, BS), 1.0, 6.0, ((0, 8),)),
    }


def block_mask(row_sizes, col_sizes):
    places = jnp.arange(BS, dtype=jnp.int32)
    rows_live = places[None, None, :] < row_sizes[:, :, None]
    cols_live = places[None, None, :] < col_sizes[:, :, None]
    return (rows_live[:, :, :, None] & cols_live[:, :, None, :]).astype(jnp.float32)

def offsets(shift_code):
    up_step = (shift_code == 2).astype(jnp.int32) - (shift_code == 1).astype(jnp.int32)
    down_step = (shift_code == 4).astype(jnp.int32) - (shift_code == 3).astype(jnp.int32)
    return (up_step, down_step)

def apply_hamiltonian(vector, left_env, right_env, term_shift, mask):
    padded = jnp.pad(vector, ((1, 1), (1, 1), (0, 0), (0, 0)))
    anchor = jnp.zeros((), jnp.int32)

    def add_term(running, channel):
        up_step, down_step = offsets(term_shift[channel])
        source = lax.dynamic_slice(padded, (1 + up_step, 1 + down_step, anchor, anchor), vector.shape)
        left_w = left_env[channel].astype(jnp.float32)
        right_w = right_env[channel].astype(jnp.float32)
        half_step = jnp.einsum('udij,udjk->udik', left_w, source.astype(jnp.float32)).astype(jnp.bfloat16)
        result = jnp.einsum('udik,udlk->udil', half_step.astype(jnp.float32), right_w)
        return (running + result, None)
    running, _ = lax.scan(add_term, jnp.zeros(vector.shape, jnp.float32), jnp.arange(W, dtype=jnp.int32))
    return running * mask

def lanczos(guess, left_env, right_env, term_shift, mask):
    start = guess.astype(jnp.float32) * mask
    norm_value = jnp.sqrt(jnp.sum(start * start))
    basis_zero = start / norm_value
    image_zero = apply_hamiltonian(basis_zero.astype(jnp.bfloat16), left_env, right_env, term_shift, mask)
    alpha_zero = jnp.sum(basis_zero * image_zero)
    residual = image_zero - alpha_zero * basis_zero
    beta_sq = jnp.sum(residual * residual)
    beta_value = jnp.sqrt(beta_sq)
    basis_one = residual / beta_value
    image_one = apply_hamiltonian(basis_one.astype(jnp.bfloat16), left_env, right_env, term_shift, mask)
    alpha_one = jnp.sum(basis_one * image_one)
    spread = 0.5 * (alpha_zero - alpha_one)
    energy = 0.5 * (alpha_zero + alpha_one) - jnp.sqrt(spread * spread + beta_value * beta_value)
    weight_zero = beta_value
    weight_one = energy - alpha_zero
    length = jnp.sqrt(weight_zero * weight_zero + weight_one * weight_one)
    ground = norm_value * (weight_zero * basis_zero + weight_one * basis_one) / length
    return (ground, energy)

def grow_env(state, env, channel_mix, factor):

    def one_channel(channel):
        half_step = jnp.einsum('udij,udjk->udik', env[channel].astype(jnp.float32), state.astype(jnp.float32)).astype(jnp.bfloat16)
        return jnp.einsum('udji,udjk->udik', state.astype(jnp.float32), half_step.astype(jnp.float32))
    blocks = lax.map(one_channel, jnp.arange(W, dtype=jnp.int32))
    return jnp.einsum('vw,wudik->vudik', channel_mix, blocks, precision=lax.Precision.HIGHEST) * factor

def reference(guess_a, guess_b, left_env_a, right_env_a, left_env_b, right_env_b, channel_mix, term_shift, sector_sizes, edge_state):
    grounds_a = []
    grounds_b = []
    energy_rows = []
    envs_a = []
    for segment in range(NSEG):
        mask_a = block_mask(sector_sizes[segment, 0], sector_sizes[segment, 1])
        mask_b = block_mask(sector_sizes[segment, 2], sector_sizes[segment, 3])
        ground_a, energy_a = lanczos(guess_a[segment], left_env_a[segment], right_env_a[segment], term_shift, mask_a)
        ground_b, energy_b = lanczos(guess_b[segment], left_env_b[segment], right_env_b[segment], term_shift, mask_b)
        grounds_a.append(ground_a)
        grounds_b.append(ground_b)
        energy_rows.append(jnp.stack([energy_a, energy_b]))
        envs_a.append(grow_env(ground_a.astype(jnp.bfloat16), left_env_a[segment], channel_mix, 1.0 / BS).astype(jnp.bfloat16))
    boundaries = []
    for segment in range(NSEG):
        if segment + 1 < NSEG:
            state = grounds_b[segment + 1].astype(jnp.bfloat16)
        else:
            state = edge_state
        boundaries.append(grow_env(state, envs_a[segment], channel_mix, 1.0 / BS).astype(jnp.bfloat16))
    return (jnp.stack(grounds_a), jnp.stack(grounds_b), jnp.stack(energy_rows), jnp.stack(boundaries))
```

```python
import functools

import jax
import jax.numpy as jnp
from jax import lax
from jax.experimental import pallas as pl
from jax.experimental.pallas import tpu as pltpu
from jax.sharding import PartitionSpec as P

F32 = jnp.float32
BF16 = jnp.bfloat16
VMEM = pl.BlockSpec(memory_space=pltpu.VMEM)
SMEM = pl.BlockSpec(memory_space=pltpu.SMEM)
ANY = pl.BlockSpec(memory_space=pl.ANY)
MIB = 1 << 20
GROUP = 16

(
    SIZE,
    QUOTIENT,
    REST,
    REST_IMAGE,
    START_IMAGE,
    REST_OWN,
    REST_LOW,
    REST_HIGH,
    START_OWN,
    START_LOW,
    START_HIGH,
) = range(11)
BOND_LANES = 64


def call(body, name, ins, outs, scratch, flops, moved, limit=24 * MIB):
    return pl.pallas_call(
        body,
        name=name,
        in_specs=ins,
        out_specs=outs[0],
        out_shape=outs[1],
        scratch_shapes=scratch,
        cost_estimate=pl.CostEstimate(flops=flops, bytes_accessed=moved, transcendentals=0),
        compiler_params=pltpu.CompilerParams(vmem_limit_bytes=limit),
    )


def live(rows, cols, block):
    row = lax.broadcasted_iota(jnp.int32, (block, block), 0)
    col = lax.broadcasted_iota(jnp.int32, (block, block), 1)
    return (row < rows) & (col < cols)


def dot(left, right):
    return jnp.dot(left, right, preferred_element_type=F32)


def dot_by_rows(left, right):
    return lax.dot_general(left, right, (((1,), (1,)), ((), ())), preferred_element_type=F32)


def dot_by_cols(left, right):
    return lax.dot_general(left, right, (((0,), (0,)), ((), ())), preferred_element_type=F32)


def total(array):
    return jnp.sum(jnp.sum(array, axis=0, keepdims=True), axis=1, keepdims=True)


def in_lanes(shape, pairs):
    lane = lax.broadcasted_iota(jnp.int32, shape, 1)
    row = jnp.zeros(shape, F32)
    for place, value in pairs:
        row = jnp.where(lane == place, value, row)
    return row


def masked_starts(sizes, guess_a, guess_b, start_a, start_b):
    downs, block = guess_a.shape[0], guess_a.shape[-1]
    for bond, (guess, start) in enumerate(((guess_a, start_a), (guess_b, start_b))):
        for down in range(downs):
            place = 2 * bond * downs + down
            mask = live(sizes[place], sizes[place + downs], block)
            start[down] = jnp.where(mask, guess[down], jnp.zeros_like(guess[down]))


def mixed_env(mix_high, mix_low, env, mixed):
    channels, downs, block = env.shape[0], env.shape[1], env.shape[-1]
    for down in range(downs):
        for group in range(block // GROUP):
            rows = slice(group * GROUP, (group + 1) * GROUP)
            part = env[:, down, rows, :].reshape(channels * GROUP, block)
            made = dot(mix_high[...], part) + dot(mix_low[...], part)
            mixed[:, down, rows, :] = made.astype(BF16).reshape(channels, GROUP, block)


def fill_sources(sources, own, low, high):
    downs = own.shape[0]
    for down in range(downs):
        sources[0, down] = own[down]
        sources[1, down] = low[down]
        sources[2, down] = high[down]
        zero = jnp.zeros(own.shape[1:], own.dtype)
        sources[3, down] = own[down - 1] if down > 0 else zero
        sources[4, down] = own[down + 1] if down + 1 < downs else zero


def first_image(bond, shift, sizes, left, right, own, low, high, rest, rest_sent, row, parts, sources):
    channels, downs, block = left.shape[0], left.shape[1], left.shape[-1]
    fill_sources(sources, own, low, high)
    parts[...] = jnp.zeros_like(parts)
    for channel in range(channels):
        code = shift[channel]
        kind = jnp.where(code <= 2, code, 0)
        for down in range(downs):
            half = dot(left[channel, down], sources[code, down]).astype(BF16)
            parts[kind, down] += dot_by_rows(half, right[channel, down])
    size = jnp.zeros((1, 1), F32)
    cross = jnp.zeros((1, 1), F32)
    for down in range(downs):
        place = 2 * bond * downs + down
        mask = live(sizes[place], sizes[place + downs], block)
        for kind in range(3):
            parts[kind, down] = jnp.where(mask, parts[kind, down], 0.0)
        image = parts[0, down] + parts[1, down] + parts[2, down]
        start = own[down].astype(F32)
        size += total(start * start)
        cross += total(start * image)
    quotient = jnp.where(size > 0.0, cross / jnp.where(size > 0.0, size, 1.0), 0.0)
    found = {place: jnp.zeros((1, 1), F32) for place in range(REST_OWN, START_HIGH + 1)}
    rest_sq = jnp.zeros((1, 1), F32)
    for down in range(downs):
        start = own[down].astype(F32)
        image = parts[0, down] + parts[1, down] + parts[2, down]
        left_over = image - quotient * start
        rest[down] = left_over
        rest_sent[down] = left_over.astype(BF16)
        rest_sq += total(left_over * left_over)
        for kind in range(3):
            found[REST_OWN + kind] += total(left_over * parts[kind, down])
            found[START_OWN + kind] += total(start * parts[kind, down])
    found[SIZE] = size
    found[QUOTIENT] = quotient
    found[REST] = rest_sq
    offset = bond * BOND_LANES
    row[...] = in_lanes(row.shape, [(offset + place, found[place]) for place in sorted(found)])


def second_image(bond, shift, left, right, own, low, high, start, rest, *refs):
    rows, out, sources = refs[:-2], refs[-2], refs[-1]
    channels, downs = left.shape[0], left.shape[1]
    fill_sources(sources, own, low, high)
    rest_image = jnp.zeros((1, 1), F32)
    start_image = jnp.zeros((1, 1), F32)
    for down in range(downs):
        image = jnp.zeros(left.shape[2:], F32)
        for channel in range(channels):
            half = dot(left[channel, down], sources[shift[channel], down]).astype(BF16)
            image = image + dot_by_rows(half, right[channel, down])
        rest_image += total(rest[down] * image)
        start_image += total(start[down].astype(F32) * image)
    offset = bond * BOND_LANES
    shape = (1, out.shape[1])
    row = in_lanes(
        shape, [(offset + REST_IMAGE, rest_image), (offset + START_IMAGE, start_image)]
    )
    for other in rows:
        row = row + other[0:1, :]
    out[...] = jnp.broadcast_to(row, out.shape)


def ritz(rows, bond):
    ups = rows.shape[0]

    def column(array, place):
        at = bond * BOND_LANES + place
        return array[:, at : at + 1]

    size = column(rows, SIZE)
    quotient = column(rows, QUOTIENT)
    norm_sq = total(size)
    alpha_zero = total(size * quotient) / norm_sq
    off = quotient - alpha_zero
    off_low = column(pltpu.roll(rows, 1, 0), QUOTIENT) - alpha_zero
    off_high = column(pltpu.roll(rows, ups - 1, 0), QUOTIENT) - alpha_zero
    residual_sq = total(column(rows, REST) + size * off * off)
    crossed = column(rows, REST_IMAGE) + off * column(rows, START_IMAGE)
    for kind, factor in enumerate((off, off_low, off_high)):
        crossed += factor * (column(rows, REST_OWN + kind) + off * column(rows, START_OWN + kind))
    alpha_one = total(crossed) / residual_sq
    beta_sq = residual_sq / norm_sq
    beta = jnp.sqrt(beta_sq)
    spread = 0.5 * (alpha_zero - alpha_one)
    energy = 0.5 * (alpha_zero + alpha_one) - jnp.sqrt(spread * spread + beta_sq)
    weight_one = energy - alpha_zero
    length = jnp.sqrt(beta_sq + weight_one * weight_one)
    of_rest = weight_one / (beta * length)
    of_start = beta / length + of_rest * off
    return energy, of_start, of_rest


def own_row(column, place):
    rows = lax.broadcasted_iota(jnp.int32, column.shape, 0)
    return total(jnp.where(rows == place, column, 0.0))


def finish(
    factor,
    ups,
    place,
    numbers,
    start_a,
    rest_a,
    start_b,
    rest_b,
    start_next,
    rest_next,
    edge,
    env,
    ground_a,
    ground_b,
    energies,
    boundary,
    made,
    sems,
):
    channels, downs = env.shape[0], env.shape[1]
    segments = numbers.shape[0] // ups
    seg, blk = place[0], place[1]
    here = numbers[pl.ds(pl.multiple_of(seg * ups, ups), ups), :]
    after = jnp.minimum(seg + 1, segments - 1)
    there = numbers[pl.ds(pl.multiple_of(after * ups, ups), ups), :]
    energy_a, a_start, a_rest = ritz(here, 0)
    energy_b, b_start, b_rest = ritz(here, 1)
    energy_next, next_start, next_rest = ritz(there, 1)
    del energy_next
    a_start, b_start, next_start = (own_row(x, blk) for x in (a_start, b_start, next_start))
    lane = lax.broadcasted_iota(jnp.int32, energies.shape, 1)
    energies[...] = jnp.where(lane == 0, energy_a, energy_b)
    last = seg == segments - 1
    products = []
    for down in range(downs):
        found_a = a_start * start_a[down].astype(F32) + a_rest * rest_a[down]
        ground_a[down] = found_a
        ground_b[down] = b_start * start_b[down].astype(F32) + b_rest * rest_b[down]
        found_next = next_start * start_next[down].astype(F32) + next_rest * rest_next[down].astype(F32)
        state = jnp.where(last, edge[down], found_next.astype(BF16))
        products.append((dot(found_a.astype(BF16), state) * factor).astype(BF16))
    copies = []
    for channel in range(channels):
        for down in range(downs):
            half = dot(env[channel, down], products[down]).astype(BF16)
            made[channel, down] = dot_by_cols(products[down], half).astype(BF16)
        copy = pltpu.make_async_copy(made.at[channel], boundary.at[channel], sems.at[channel])
        copy.start()
        copies.append(copy)
    for copy in copies:
        copy.wait()


def passed_along(block, axis, distance):
    devices = range(lax.axis_size(axis))
    route = [(i - distance, i) for i in devices if i - distance in devices]
    return lax.ppermute(block, axis, route)


def local(
    guess_a,
    guess_b,
    left_env_a,
    right_env_a,
    left_env_b,
    right_env_b,
    channel_mix,
    term_shift,
    sector_sizes,
    edge_state,
):
    block = guess_a.shape[-1]
    downs = guess_a.shape[2]
    channels = left_env_a.shape[1]
    ups = lax.axis_size("blk")
    segments = lax.axis_size("seg")
    devices = ups * segments
    pair = (downs, block, block)
    env_shape = (channels, downs, block, block)
    lefts = [left_env_a.reshape(env_shape), left_env_b.reshape(env_shape)]
    rights = [right_env_a.reshape(env_shape), right_env_b.reshape(env_shape)]
    sizes = sector_sizes.reshape(-1)
    bits = 2 * downs * block * block
    env_bytes = channels * bits
    apply_flops = 4 * channels * downs * block**3
    state16 = jax.ShapeDtypeStruct(pair, BF16)
    state32 = jax.ShapeDtypeStruct(pair, F32)

    starts = call(
        masked_starts,
        "masked_starts",
        [SMEM, VMEM, VMEM],
        ((VMEM, VMEM), (state16, state16)),
        [],
        4 * downs * block * block,
        4 * bits,
    )(sizes, guess_a.reshape(pair), guess_b.reshape(pair))
    lows = [passed_along(start, "blk", 1) for start in starts]
    highs = [passed_along(start, "blk", -1) for start in starts]
    start_next = passed_along(starts[1], "seg", -1)

    squared = jnp.dot(channel_mix, channel_mix, precision=lax.Precision.HIGHEST)
    spread = (squared[:, None, :, None] * jnp.eye(GROUP, dtype=F32)[None, :, None, :]).reshape(
        channels * GROUP, channels * GROUP
    )
    mix_high = spread.astype(BF16)
    mix_low = (spread - mix_high.astype(F32)).astype(BF16)
    env = call(
        mixed_env,
        "mixed_env",
        [VMEM] * 3,
        (VMEM, jax.ShapeDtypeStruct(env_shape, BF16)),
        [],
        4 * channels * channels * GROUP * downs * block * block,
        2 * env_bytes,
    )(mix_high, mix_low, lefts[0])

    rests, rests_sent, rows = [], [], []
    for bond in range(2):
        rest, rest_sent, row = call(
            functools.partial(first_image, bond),
            f"first_image_{bond}",
            [SMEM, SMEM] + [VMEM] * 5,
            ((VMEM,) * 3, (state32, state16, jax.ShapeDtypeStruct((8, 128), F32))),
            [pltpu.VMEM((3,) + pair, F32), pltpu.VMEM((5,) + pair, BF16)],
            apply_flops,
            2 * env_bytes,
        )(term_shift, sizes, lefts[bond], rights[bond], starts[bond], lows[bond], highs[bond])
        rests.append(rest)
        rests_sent.append(rest_sent)
        rows.append(row)
    rest_lows = [passed_along(rest, "blk", 1) for rest in rests_sent]
    rest_highs = [passed_along(rest, "blk", -1) for rest in rests_sent]
    rest_next = passed_along(rests_sent[1], "seg", -1)
    for bond in range(2):
        rows_in = rows if bond == 1 else []
        height = devices if bond == 1 else 8
        row = call(
            functools.partial(second_image, bond),
            f"second_image_{bond}",
            [SMEM] + [VMEM] * (7 + len(rows_in)),
            (VMEM, jax.ShapeDtypeStruct((height, 128), F32)),
            [pltpu.VMEM((5,) + pair, BF16)],
            apply_flops,
            2 * env_bytes,
        )(
            term_shift,
            lefts[bond],
            rights[bond],
            rests_sent[bond],
            rest_lows[bond],
            rest_highs[bond],
            starts[bond],
            rests[bond],
            *rows_in,
        )
        rows.append(row)
    numbers = lax.all_to_all(rows[-1], ("seg", "blk"), 0, 0, tiled=True)
    place = jnp.stack([lax.axis_index("seg"), lax.axis_index("blk")]).astype(jnp.int32)
    ground_a, ground_b, energies, boundary = call(
        functools.partial(finish, 1.0 / block, ups),
        "finish",
        [SMEM] + [VMEM] * 9,
        (
            (VMEM, VMEM, VMEM, ANY),
            (
                state32,
                state32,
                jax.ShapeDtypeStruct((1, 2), F32),
                jax.ShapeDtypeStruct(env_shape, BF16),
            ),
        ),
        [pltpu.VMEM(env_shape, BF16), pltpu.SemaphoreType.DMA((channels,))],
        apply_flops,
        2 * env_bytes,
    )(
        place,
        numbers,
        starts[0],
        rests[0],
        starts[1],
        rests[1],
        start_next,
        rest_next,
        edge_state.reshape(pair),
        env,
    )
    return (
        ground_a.reshape(guess_a.shape),
        ground_b.reshape(guess_b.shape),
        energies,
        boundary.reshape(left_env_a.shape),
    )


def solution(mesh):
    placed = (
        P("seg", "blk", None, None, None),
        P("seg", "blk", None, None, None),
        P("seg", None, "blk", None, None, None),
        P("seg", None, "blk", None, None, None),
        P("seg", None, "blk", None, None, None),
        P("seg", None, "blk", None, None, None),
        P(),
        P(),
        P("seg", None, "blk", None),
        P("blk", None, None, None),
    )
    return jax.shard_map(
        local,
        mesh=mesh,
        in_specs=placed,
        out_specs=(
            P("seg", "blk", None, None, None),
            P("seg", "blk", None, None, None),
            P("seg", None),
            P("seg", None, "blk", None, None, None),
        ),
        check_vma=False,
    )
```

```python
import functools

import jax
import jax.numpy as jnp
from jax import lax
from jax.experimental import pallas as pl
from jax.experimental.pallas import tpu as pltpu
from jax.sharding import PartitionSpec as P

F32 = jnp.float32
BF16 = jnp.bfloat16
VMEM = pl.BlockSpec(memory_space=pltpu.VMEM)
SMEM = pl.BlockSpec(memory_space=pltpu.SMEM)
HBM = pl.BlockSpec(memory_space=pltpu.HBM)
MIB = 1 << 20
GROUP = 16
BATCH = 3
BONDS = 2
CODES = 5

(
    SIZE,
    QUOTIENT,
    REST,
    REST_IMAGE,
    START_IMAGE,
    REST_OWN,
    REST_LOW,
    REST_HIGH,
    START_OWN,
    START_LOW,
    START_HIGH,
) = range(11)
BOND_LANES = 64


def call(body, name, ins, outs, scratch, flops, moved, limit=20 * MIB):
    return pl.pallas_call(
        body,
        name=name,
        in_specs=ins,
        out_specs=tuple(spec for spec, _ in outs),
        out_shape=tuple(shape for _, shape in outs),
        scratch_shapes=scratch,
        cost_estimate=pl.CostEstimate(flops=flops, bytes_accessed=moved, transcendentals=0),
        compiler_params=pltpu.CompilerParams(vmem_limit_bytes=limit),
    )


def in_hbm(array):
    return pltpu.with_memory_space_constraint(array, pltpu.HBM)


def live(rows, cols, block):
    row = lax.broadcasted_iota(jnp.int32, (block, block), 0)
    col = lax.broadcasted_iota(jnp.int32, (block, block), 1)
    return (row < rows) & (col < cols)


def live_of(sizes, bond, down, block):
    return live(sizes[0, 0, down, 2 * bond], sizes[0, 0, down, 2 * bond + 1], block)


def dot(left, right):
    return jnp.dot(left, right, preferred_element_type=F32)


def dot_by_rows(left, right):
    return lax.dot_general(left, right, (((1,), (1,)), ((), ())), preferred_element_type=F32)


def exact_dot(left, right):
    return jnp.dot(left, right, precision=lax.Precision.HIGHEST, preferred_element_type=F32)


def total(array):
    return jnp.sum(jnp.sum(array, axis=0, keepdims=True), axis=1, keepdims=True)


def in_lanes(width, pairs):
    lane = lax.broadcasted_iota(jnp.int32, (1, width), 1)
    row = jnp.zeros((1, width), F32)
    for place, value in pairs:
        row = jnp.where(lane == place, value, row)
    return row


def masked_starts(sizes, guess_a, guess_b, starts, sems):
    copies = [
        pltpu.make_async_copy(guess, starts.at[bond], sems.at[bond])
        for bond, guess in enumerate((guess_a, guess_b))
    ]
    for copy in copies:
        copy.start()
    downs, block = starts.shape[1], starts.shape[-1]
    for bond in range(BONDS):
        copies[bond].wait()
        for down in range(downs):
            start = starts[bond, down]
            starts[bond, down] = jnp.where(
                live_of(sizes, bond, down, block), start, jnp.zeros_like(start)
            )


def list_channels(shift, lists):
    channels = shift.shape[0]
    for code in range(CODES):
        count = jnp.int32(0)
        for channel in range(channels):
            lists[code, count] = jnp.int32(channel)
            count = count + (shift[channel] == code).astype(jnp.int32)
        lists[code, channels] = count


def add_images(lists, code, lefts, rights, sources, sums, arrived=None):
    channels = lefts[0].shape[0]
    downs = lefts[0].shape[1]
    units = [
        (bond, down)
        for bond in range(BONDS)
        for down in range(downs)
        if sources(bond, down) is not None
    ]

    def step(index, carry):
        channel = lists[code, index]
        if arrived is not None:
            arrived(channel)
        halves = [
            dot(lefts[bond][channel, down], sources(bond, down)[...]).astype(BF16)
            for bond, down in units
        ]
        for (bond, down), half in zip(units, halves):
            sums[bond, down] += dot_by_rows(half, rights[bond][channel, down])
        return carry

    lax.fori_loop(0, lists[code, channels], step, 0)


def add_local_images(lists, lefts, rights, states, sums, arrived=None):
    downs = states.shape[1]

    def below(bond, down):
        return states.at[bond, down - 1] if down > 0 else None

    def above(bond, down):
        return states.at[bond, down + 1] if down + 1 < downs else None

    add_images(lists, 0, lefts, rights, lambda bond, down: states.at[bond, down], sums, arrived)
    add_images(lists, 3, lefts, rights, below, sums, arrived)
    add_images(lists, 4, lefts, rights, above, sums, arrived)


def add_halo_images(lists, lefts, rights, swapped, shifted, halo, sums_low, sums_high):
    even = lax.rem(lax.axis_index("blk"), 2) == 0
    downs = swapped.shape[1]
    for bond in range(BONDS):
        for down in range(downs):
            one, other = swapped[bond, down], shifted[bond, down]
            halo[0, bond, down] = jnp.where(even, other, one)
            halo[1, bond, down] = jnp.where(even, one, other)
    add_images(lists, 1, lefts, rights, lambda bond, down: halo.at[0, bond, down], sums_low)
    add_images(lists, 2, lefts, rights, lambda bond, down: halo.at[1, bond, down], sums_high)


def opening(shift, starts, *refs):
    held, loaded, (own_images, lists, sems) = refs[:4], refs[4:8], refs[8:]
    left_a, right_a, left_b, right_b = loaded
    channels = left_a.shape[0]
    list_channels(shift, lists)

    def copies(channel):
        return [
            pltpu.make_async_copy(source.at[channel], target.at[channel], sems.at[channel])
            for source, target in zip(held, loaded)
        ]

    def bring(index, carry, code):
        for copy in copies(lists[code, index]):
            copy.start()
        return carry

    def await_one(channel):
        for copy in copies(channel):
            copy.wait()

    def await_listed(index, carry, code):
        await_one(lists[code, index])
        return carry

    for code in (0, 3, 4, 1, 2):
        lax.fori_loop(0, lists[code, channels], functools.partial(bring, code=code), 0)
    own_images[...] = jnp.zeros_like(own_images)
    add_local_images(lists, (left_a, left_b), (right_a, right_b), starts, own_images, await_one)
    for code in (1, 2):
        lax.fori_loop(0, lists[code, channels], functools.partial(await_listed, code=code), 0)


def mixing(mix, env, after, mixed):
    del after
    channels, downs, block = env.shape[0], env.shape[1], env.shape[-1]
    wide = channels * GROUP
    squared = exact_dot(mix[...], mix[...])
    spread_rows = (
        lax.broadcasted_iota(jnp.int32, (wide, channels), 0) // GROUP
        == lax.broadcasted_iota(jnp.int32, (wide, channels), 1)
    ).astype(F32)
    spread_cols = (
        lax.broadcasted_iota(jnp.int32, (channels, wide), 1) // GROUP
        == lax.broadcasted_iota(jnp.int32, (channels, wide), 0)
    ).astype(F32)
    spread = exact_dot(exact_dot(spread_rows, squared), spread_cols)
    same = lax.rem(lax.broadcasted_iota(jnp.int32, (wide, wide), 0), GROUP) == lax.rem(
        lax.broadcasted_iota(jnp.int32, (wide, wide), 1), GROUP
    )
    spread = jnp.where(same, spread, 0.0)
    mix_high = spread.astype(BF16)
    mix_low = (spread - mix_high.astype(F32)).astype(BF16)
    for down in range(downs):
        for group in range(block // GROUP):
            rows = slice(group * GROUP, (group + 1) * GROUP)
            part = env[:, down, rows, :].reshape(wide, block)
            made = dot(mix_high, part) + dot(mix_low, part)
            mixed[:, down, rows, :] = made.astype(BF16).reshape(channels, GROUP, block)


def first_images(
    lists,
    sizes,
    left_a,
    right_a,
    left_b,
    right_b,
    starts,
    swapped,
    shifted,
    own_images,
    rest,
    sent,
    along,
    halo_images,
    row,
    halo,
):
    downs, block = left_a.shape[1], left_a.shape[-1]
    halo_images[...] = jnp.zeros_like(halo_images)
    add_halo_images(
        lists,
        (left_a, left_b),
        (right_a, right_b),
        swapped,
        shifted,
        halo,
        halo_images.at[0],
        halo_images.at[1],
    )
    found = []
    for bond in range(BONDS):
        size = jnp.zeros((1, 1), F32)
        cross = jnp.zeros((1, 1), F32)
        for down in range(downs):
            image = own_images[bond, down] + halo_images[0, bond, down] + halo_images[1, bond, down]
            rest[bond, down] = image
            start = starts[bond, down].astype(F32)
            size += total(start * start)
            cross += total(start * image)
        quotient = jnp.where(size > 0.0, cross / jnp.where(size > 0.0, size, 1.0), 0.0)
        for down in range(downs):
            image = jnp.where(live_of(sizes, bond, down, block), rest[bond, down], 0.0)
            left_over = image - quotient * starts[bond, down].astype(F32)
            rest[bond, down] = left_over
            sent[bond, down] = left_over.astype(BF16)
        offset = bond * BOND_LANES
        found += [(offset + SIZE, size), (offset + QUOTIENT, quotient)]
    along[0] = starts[BONDS - 1]
    along[1] = sent[BONDS - 1]
    row[...] = jnp.broadcast_to(in_lanes(row.shape[1], found), row.shape)


def local_seconds(
    lists,
    left_a,
    right_a,
    left_b,
    right_b,
    sent,
    starts,
    rest,
    own_images,
    halo_images,
    row_in,
    row,
    sums,
):
    downs = left_a.shape[1]
    sums[...] = jnp.zeros_like(sums)
    add_local_images(lists, (left_a, left_b), (right_a, right_b), sent, sums)
    found = []
    for bond in range(BONDS):
        numbers = {place: jnp.zeros((1, 1), F32) for place in range(REST, START_HIGH + 1)}
        for down in range(downs):
            start = starts[bond, down].astype(F32)
            left_over = rest[bond, down]
            numbers[REST] += total(left_over * left_over)
            numbers[REST_IMAGE] += total(left_over * sums[bond, down])
            numbers[START_IMAGE] += total(start * sums[bond, down])
            parts = (own_images[bond, down], halo_images[0, bond, down], halo_images[1, bond, down])
            for kind, part in enumerate(parts):
                numbers[REST_OWN + kind] += total(left_over * part)
                numbers[START_OWN + kind] += total(start * part)
        offset = bond * BOND_LANES
        found += [(offset + place, numbers[place]) for place in sorted(numbers)]
    row[...] = row_in[...] + jnp.broadcast_to(in_lanes(row.shape[1], found), row.shape)


def halo_seconds(
    lists,
    left_a,
    right_a,
    left_b,
    right_b,
    swapped,
    shifted,
    starts,
    rest,
    row_in,
    row,
    halo,
    sums,
):
    downs = left_a.shape[1]
    sums[...] = jnp.zeros_like(sums)
    add_halo_images(
        lists, (left_a, left_b), (right_a, right_b), swapped, shifted, halo, sums, sums
    )
    found = []
    for bond in range(BONDS):
        of_rest = jnp.zeros((1, 1), F32)
        of_start = jnp.zeros((1, 1), F32)
        for down in range(downs):
            of_rest += total(rest[bond, down] * sums[bond, down])
            of_start += total(starts[bond, down].astype(F32) * sums[bond, down])
        offset = bond * BOND_LANES
        found += [(offset + REST_IMAGE, of_rest), (offset + START_IMAGE, of_start)]
    row[...] = jnp.broadcast_to(row_in[0:1, :] + in_lanes(row.shape[1], found), row.shape)


def ritz(rows):
    ups = rows.shape[1]

    def column(array, place):
        return array[:, :, place : place + 1]

    def over_ups(array):
        return jnp.sum(array, axis=1, keepdims=True)

    size = column(rows, SIZE)
    quotient = column(rows, QUOTIENT)
    norm_sq = over_ups(size)
    alpha_zero = over_ups(size * quotient) / norm_sq
    off = quotient - alpha_zero
    off_low = column(pltpu.roll(rows, 1, 1), QUOTIENT) - alpha_zero
    off_high = column(pltpu.roll(rows, ups - 1, 1), QUOTIENT) - alpha_zero
    residual_sq = over_ups(column(rows, REST) + size * off * off)
    crossed = column(rows, REST_IMAGE) + off * column(rows, START_IMAGE)
    for kind, factor in enumerate((off, off_low, off_high)):
        crossed += factor * (column(rows, REST_OWN + kind) + off * column(rows, START_OWN + kind))
    alpha_one = over_ups(crossed) / residual_sq
    beta_sq = residual_sq / norm_sq
    beta = jnp.sqrt(beta_sq)
    spread = 0.5 * (alpha_zero - alpha_one)
    energy = 0.5 * (alpha_zero + alpha_one) - jnp.sqrt(spread * spread + beta_sq)
    weight_one = energy - alpha_zero
    length = jnp.sqrt(beta_sq + weight_one * weight_one)
    of_rest = weight_one / (beta * length)
    of_start = beta / length + of_rest * off
    return energy, of_start, of_rest


def finish(
    factor,
    ups,
    numbers,
    starts_held,
    rest_held,
    along_held,
    edge_held,
    mixed_held,
    ground_a,
    ground_b,
    energies,
    boundary,
    starts,
    rest,
    along,
    edge,
    mixed,
    made,
    grounds,
    in_sems,
    mixed_sems,
    out_sems,
):
    channels, downs = mixed.shape[0], mixed.shape[1]
    held = ((starts_held, starts), (rest_held, rest), (along_held, along), (edge_held, edge))
    arrivals = [
        pltpu.make_async_copy(source, target, in_sems.at[index])
        for index, (source, target) in enumerate(held)
    ]
    arrivals += [
        pltpu.make_async_copy(mixed_held.at[index], mixed.at[index], mixed_sems.at[index])
        for index in range(channels)
    ]
    for copy in arrivals:
        copy.start()
    segments = numbers.shape[0] // ups
    seg, blk = lax.axis_index("seg"), lax.axis_index("blk")
    here = numbers[pl.ds(pl.multiple_of(seg * ups, ups), ups), :]
    after = jnp.minimum(seg + 1, segments - 1)
    there = numbers[pl.ds(pl.multiple_of(after * ups, ups), ups), :]
    width = numbers.shape[1]
    energy, of_start, of_rest = ritz(
        jnp.stack(
            [
                here,
                pltpu.roll(here, width - BOND_LANES, 1),
                pltpu.roll(there, width - BOND_LANES, 1),
            ]
        )
    )
    place = lax.broadcasted_iota(jnp.int32, of_start.shape, 1)
    of_start = jnp.sum(jnp.where(place == blk, of_start, 0.0), axis=1, keepdims=True)
    lane = lax.broadcasted_iota(jnp.int32, energies.shape, 1)
    energies[...] = jnp.where(lane == 0, energy[0], energy[1])
    last = seg == segments - 1
    for copy in arrivals[:2]:
        copy.wait()
    for bond in range(BONDS):
        for down in range(downs):
            start = starts[bond, down].astype(F32)
            grounds[bond, down] = of_start[bond] * start + of_rest[bond] * rest[bond, down]
    copies = [
        pltpu.make_async_copy(grounds.at[bond], target, out_sems.at[channels + bond])
        for bond, target in enumerate((ground_a, ground_b))
    ]
    for copy in copies:
        copy.start()
    for copy in arrivals[2:4]:
        copy.wait()
    products = []
    for down in range(downs):
        found = of_start[2] * along[0, down].astype(F32) + of_rest[2] * along[1, down].astype(F32)
        state = jnp.where(last, edge[down], found.astype(BF16))
        product = dot(grounds[0, down].astype(BF16), state) * factor
        products.append((product.astype(BF16), product.T.astype(BF16)))
    halves = {}

    def last_product(group):
        for channel in group:
            for down, (_, turned) in enumerate(products):
                made[channel, down] = dot(turned, halves[channel, down]).astype(BF16)
        for channel in group:
            copy = pltpu.make_async_copy(
                made.at[channel], boundary.at[channel], out_sems.at[channel]
            )
            copy.start()
            copies.append(copy)

    groups = [range(i, min(i + BATCH, channels)) for i in range(0, channels, BATCH)]
    for index, group in enumerate(groups):
        for channel in group:
            arrivals[4 + channel].wait()
        for channel in group:
            for down, (product, _) in enumerate(products):
                halves[channel, down] = dot(mixed[channel, down], product).astype(BF16)
        if index > 0:
            last_product(groups[index - 1])
    last_product(groups[-1])
    for copy in copies:
        copy.wait()


def swapped_pairs(block):
    devices = range(lax.axis_size("blk"))
    return lax.ppermute(block, "blk", [(i, i ^ 1) for i in devices if i ^ 1 in devices])


def shifted_pairs(block):
    devices = range(lax.axis_size("blk"))
    pairs = [(i, i + 1) for i in devices if i % 2 == 1 and i + 1 in devices]
    return lax.ppermute(block, "blk", pairs + [(j, i) for i, j in pairs])


def from_right_segment(block):
    segments = lax.axis_size("seg")
    return lax.ppermute(block, "seg", [(i + 1, i) for i in range(segments - 1)])


def local(
    guess_a,
    guess_b,
    left_env_a,
    right_env_a,
    left_env_b,
    right_env_b,
    channel_mix,
    term_shift,
    sector_sizes,
    edge_state,
):
    block = guess_a.shape[-1]
    downs = guess_a.shape[2]
    channels = left_env_a.shape[1]
    ups = lax.axis_size("blk")
    devices = ups * lax.axis_size("seg")
    pair = (downs, block, block)
    both = (BONDS,) + pair
    env_shape = (channels, downs, block, block)
    held = [in_hbm(env.reshape(env_shape)) for env in (left_env_a, right_env_a, left_env_b, right_env_b)]
    bits = 2 * downs * block * block
    env_bytes = channels * bits
    apply_flops = 4 * channels * downs * block**3
    sizes = in_hbm(sector_sizes.transpose(0, 2, 3, 1))
    tile = jax.ShapeDtypeStruct((8, 128), F32)

    (starts,) = call(
        masked_starts,
        "masked_starts",
        [SMEM, HBM, HBM],
        [(VMEM, pltpu.VMEM(both, BF16))],
        [pltpu.SemaphoreType.DMA((2,))],
        4 * downs * block * block,
        4 * bits,
    )(sizes, in_hbm(guess_a.reshape(pair)), in_hbm(guess_b.reshape(pair)))
    shifted, swapped = shifted_pairs(starts), swapped_pairs(starts)

    *loaded, own_images, lists = call(
        opening,
        "opening",
        [SMEM, VMEM] + [HBM] * 4,
        [(VMEM, pltpu.VMEM(env_shape, BF16))] * 4
        + [
            (VMEM, pltpu.VMEM(both, F32)),
            (SMEM, jax.ShapeDtypeStruct((CODES, channels + 1), jnp.int32)),
        ],
        [pltpu.SemaphoreType.DMA((channels,))],
        apply_flops,
        5 * env_bytes,
    )(in_hbm(term_shift), starts, *held)

    halo = pltpu.VMEM((2,) + both, BF16)
    rest, sent, along, halo_images, row = call(
        first_images,
        "first_images",
        [SMEM, SMEM] + [VMEM] * 8,
        [
            (VMEM, pltpu.VMEM(both, F32)),
            (VMEM, pltpu.VMEM(both, BF16)),
            (VMEM, pltpu.VMEM((2,) + pair, BF16)),
            (VMEM, pltpu.VMEM((2,) + both, F32)),
            (VMEM, tile),
        ],
        [halo],
        apply_flops,
        env_bytes,
    )(lists, sizes, *loaded, starts, swapped, shifted, own_images)
    shifted, swapped = shifted_pairs(sent), swapped_pairs(sent)
    from_next = from_right_segment(along)
    (row,) = call(
        local_seconds,
        "local_seconds",
        [SMEM] + [VMEM] * 10,
        [(VMEM, tile)],
        [pltpu.VMEM(both, F32)],
        apply_flops,
        env_bytes,
    )(lists, *loaded, sent, starts, rest, own_images, halo_images, row)
    (row,) = call(
        halo_seconds,
        "halo_seconds",
        [SMEM] + [VMEM] * 9,
        [(VMEM, jax.ShapeDtypeStruct((devices, 128), F32))],
        [halo, pltpu.VMEM(both, F32)],
        apply_flops,
        env_bytes,
    )(lists, *loaded, swapped, shifted, starts, rest, row)
    numbers = lax.all_to_all(row, ("seg", "blk"), 0, 0, tiled=True)
    (mixed,) = call(
        mixing,
        "mixing",
        [VMEM, VMEM, HBM],
        [(VMEM, jax.ShapeDtypeStruct(env_shape, BF16))],
        [],
        4 * channels * channels * GROUP * downs * block * block,
        2 * env_bytes,
    )(channel_mix, loaded[0], row)
    state32 = jax.ShapeDtypeStruct(pair, F32)
    ground_a, ground_b, energies, boundary = call(
        functools.partial(finish, 1.0 / block, ups),
        "finish",
        [VMEM] + [HBM] * 5,
        [
            (HBM, state32),
            (HBM, state32),
            (VMEM, jax.ShapeDtypeStruct((1, 2), F32)),
            (HBM, jax.ShapeDtypeStruct(env_shape, BF16)),
        ],
        [
            pltpu.VMEM(both, BF16),
            pltpu.VMEM(both, F32),
            pltpu.VMEM((2,) + pair, BF16),
            pltpu.VMEM(pair, BF16),
            pltpu.VMEM(env_shape, BF16),
            pltpu.VMEM(env_shape, BF16),
            pltpu.VMEM(both, F32),
            pltpu.SemaphoreType.DMA((4,)),
            pltpu.SemaphoreType.DMA((channels,)),
            pltpu.SemaphoreType.DMA((channels + BONDS,)),
        ],
        apply_flops,
        2 * env_bytes,
    )(
        numbers,
        *(in_hbm(x) for x in (starts, rest, from_next, edge_state.reshape(pair), mixed)),
    )
    return (
        ground_a.reshape(guess_a.shape),
        ground_b.reshape(guess_b.shape),
        energies,
        boundary.reshape(left_env_a.shape),
    )


def solution(mesh):
    placed = (
        P("seg", "blk", None, None, None),
        P("seg", "blk", None, None, None),
        P("seg", None, "blk", None, None, None),
        P("seg", None, "blk", None, None, None),
        P("seg", None, "blk", None, None, None),
        P("seg", None, "blk", None, None, None),
        P(),
        P(),
        P("seg", None, "blk", None),
        P("blk", None, None, None),
    )
    return jax.shard_map(
        local,
        mesh=mesh,
        in_specs=placed,
        out_specs=(
            P("seg", "blk", None, None, None),
            P("seg", "blk", None, None, None),
            P("seg", None),
            P("seg", None, "blk", None, None, None),
        ),
        check_vma=False,
    )
```

```python
import functools

import jax
import jax.numpy as jnp
from jax import lax
from jax.experimental import pallas as pl
from jax.experimental.pallas import tpu as pltpu
from jax.sharding import PartitionSpec as P

F32 = jnp.float32
BF16 = jnp.bfloat16
VMEM = pl.BlockSpec(memory_space=pltpu.VMEM)
SMEM = pl.BlockSpec(memory_space=pltpu.SMEM)
HBM = pl.BlockSpec(memory_space=pltpu.HBM)
MIB = 1 << 20
GROUP = 16
BATCH = 3
BONDS = 2
CODES = 5
HALO_CHANNELS, HALO_KINDS = CODES, CODES + 1

(
    SIZE,
    QUOTIENT,
    REST,
    REST_IMAGE,
    START_IMAGE,
    REST_OWN,
    REST_LOW,
    REST_HIGH,
    START_OWN,
    START_LOW,
    START_HIGH,
) = range(11)
BOND_LANES = 64


def call(body, name, ins, outs, scratch, flops, moved, limit=20 * MIB):
    return pl.pallas_call(
        body,
        name=name,
        in_specs=ins,
        out_specs=tuple(spec for spec, _ in outs),
        out_shape=tuple(shape for _, shape in outs),
        scratch_shapes=scratch,
        cost_estimate=pl.CostEstimate(flops=flops, bytes_accessed=moved, transcendentals=0),
        compiler_params=pltpu.CompilerParams(vmem_limit_bytes=limit),
    )


def in_hbm(array):
    return pltpu.with_memory_space_constraint(array, pltpu.HBM)


def live(rows, cols, block):
    row = lax.broadcasted_iota(jnp.int32, (block, block), 0)
    col = lax.broadcasted_iota(jnp.int32, (block, block), 1)
    return (row < rows) & (col < cols)


def live_of(sizes, bond, down, block):
    return live(sizes[0, 0, down, 2 * bond], sizes[0, 0, down, 2 * bond + 1], block)


def dot(left, right):
    return jnp.dot(left, right, preferred_element_type=F32)


def dot_by_rows(left, right):
    return lax.dot_general(left, right, (((1,), (1,)), ((), ())), preferred_element_type=F32)


def exact_dot(left, right):
    return jnp.dot(left, right, precision=lax.Precision.HIGHEST, preferred_element_type=F32)


def total(array):
    return jnp.sum(jnp.sum(array, axis=0, keepdims=True), axis=1, keepdims=True)


def in_lanes(width, pairs):
    lane = lax.broadcasted_iota(jnp.int32, (1, width), 1)
    row = jnp.zeros((1, width), F32)
    for place, value in pairs:
        row = jnp.where(lane == place, value, row)
    return row


def masked_starts(sizes_held, guess_a, guess_b, starts, sizes, size_sem, sems):
    sizes_copy = pltpu.make_async_copy(sizes_held, sizes, size_sem)
    sizes_copy.start()
    downs, block = starts.shape[1], starts.shape[-1]
    places = [(bond, down) for bond in range(BONDS) for down in range(downs)]
    copies = [
        pltpu.make_async_copy(
            (guess_a, guess_b)[bond].at[down], starts.at[bond, down], sems.at[bond, down]
        )
        for bond, down in places
    ]
    for copy in copies:
        copy.start()
    sizes_copy.wait()
    for copy, (bond, down) in zip(copies, places):
        copy.wait()
        start = starts[bond, down]
        starts[bond, down] = jnp.where(
            live_of(sizes, bond, down, block), start, jnp.zeros_like(start)
        )


def list_channels(shift, lists):
    channels = shift.shape[0]
    for code in range(CODES):
        count = jnp.int32(0)
        for channel in range(channels):
            lists[code, count] = jnp.int32(channel)
            count = count + (shift[channel] == code).astype(jnp.int32)
        lists[code, channels] = count
    count = jnp.int32(0)
    for channel in range(channels):
        code = shift[channel]
        lists[HALO_CHANNELS, count] = jnp.int32(channel)
        lists[HALO_KINDS, count] = (code == 2).astype(jnp.int32)
        count = count + ((code == 1) | (code == 2)).astype(jnp.int32)
    lists[HALO_CHANNELS, channels] = count


def add_images(lists, code, lefts, rights, sources, sums, arrived=None):
    channels = lefts[0].shape[0]
    downs = lefts[0].shape[1]
    units = [
        (bond, down)
        for bond in range(BONDS)
        for down in range(downs)
        if sources(bond, down) is not None
    ]

    def step(index, carry):
        channel = lists[code, index]
        if arrived is not None:
            arrived(channel)
        halves = [
            dot(lefts[bond][channel, down], sources(bond, down)[...]).astype(BF16)
            for bond, down in units
        ]
        for (bond, down), half in zip(units, halves):
            sums[bond, down] += dot_by_rows(half, rights[bond][channel, down])
        return carry

    lax.fori_loop(0, lists[code, channels], step, 0)


def add_local_images(lists, lefts, rights, states, sums, arrived=None):
    downs = states.shape[1]

    def below(bond, down):
        return states.at[bond, down - 1] if down > 0 else None

    def above(bond, down):
        return states.at[bond, down + 1] if down + 1 < downs else None

    add_images(lists, 0, lefts, rights, lambda bond, down: states.at[bond, down], sums, arrived)
    add_images(lists, 3, lefts, rights, below, sums, arrived)
    add_images(lists, 4, lefts, rights, above, sums, arrived)


def add_halo_images(lists, lefts, rights, swapped, shifted, halo, sums, parted, lists_copy):
    even = lax.rem(lax.axis_index("blk"), 2) == 0
    channels = lefts[0].shape[0]
    downs = swapped.shape[1]
    units = [(bond, down) for bond in range(BONDS) for down in range(downs)]
    for bond, down in units:
        one, other = swapped[bond, down], shifted[bond, down]
        halo[0, bond, down] = jnp.where(even, other, one)
        halo[1, bond, down] = jnp.where(even, one, other)
    lists_copy.wait()

    def images(indices):
        halves = []
        for index in indices:
            channel, kind = lists[HALO_CHANNELS, index], lists[HALO_KINDS, index]
            halves.append(
                [
                    dot(lefts[bond][channel, down], halo[kind, bond, down]).astype(BF16)
                    for bond, down in units
                ]
            )
        for index, half_steps in zip(indices, halves):
            channel, kind = lists[HALO_CHANNELS, index], lists[HALO_KINDS, index]
            target = sums.at[kind] if parted else sums
            for (bond, down), half in zip(units, half_steps):
                target[bond, down] += dot_by_rows(half, rights[bond][channel, down])

    def two(index, carry):
        images([2 * index, 2 * index + 1])
        return carry

    def one_left(index, carry):
        images([index])
        return carry

    count = lists[HALO_CHANNELS, channels]
    odd = lax.rem(count, 2)
    lax.fori_loop(0, lax.div(count, 2), two, 0)
    lax.fori_loop(count - odd, count, one_left, 0)


def opening(shift, starts, *refs):
    held, loaded, (own_images, lists, sems) = refs[:4], refs[4:8], refs[8:]
    left_a, right_a, left_b, right_b = loaded
    channels = left_a.shape[0]
    list_channels(shift, lists)

    def copies(channel):
        return [
            pltpu.make_async_copy(source.at[channel], target.at[channel], sems.at[channel])
            for source, target in zip(held, loaded)
        ]

    def bring(index, carry, code):
        for copy in copies(lists[code, index]):
            copy.start()
        return carry

    def await_one(channel):
        for copy in copies(channel):
            copy.wait()

    def await_listed(index, carry, code):
        await_one(lists[code, index])
        return carry

    for code in (0, 3, 4, 1, 2):
        lax.fori_loop(0, lists[code, channels], functools.partial(bring, code=code), 0)
    own_images[...] = jnp.zeros_like(own_images)
    add_local_images(lists, (left_a, left_b), (right_a, right_b), starts, own_images, await_one)
    for code in (1, 2):
        lax.fori_loop(0, lists[code, channels], functools.partial(await_listed, code=code), 0)


def mixing(mix, env, after, mixed):
    del after
    channels, downs, block = env.shape[0], env.shape[1], env.shape[-1]
    wide = channels * GROUP
    squared = exact_dot(mix[...], mix[...])
    spread_rows = (
        lax.broadcasted_iota(jnp.int32, (wide, channels), 0) // GROUP
        == lax.broadcasted_iota(jnp.int32, (wide, channels), 1)
    ).astype(F32)
    spread_cols = (
        lax.broadcasted_iota(jnp.int32, (channels, wide), 1) // GROUP
        == lax.broadcasted_iota(jnp.int32, (channels, wide), 0)
    ).astype(F32)
    spread = exact_dot(exact_dot(spread_rows, squared), spread_cols)
    same = lax.rem(lax.broadcasted_iota(jnp.int32, (wide, wide), 0), GROUP) == lax.rem(
        lax.broadcasted_iota(jnp.int32, (wide, wide), 1), GROUP
    )
    spread = jnp.where(same, spread, 0.0)
    mix_high = spread.astype(BF16)
    mix_low = (spread - mix_high.astype(F32)).astype(BF16)
    for down in range(downs):
        for group in range(block // GROUP):
            rows = slice(group * GROUP, (group + 1) * GROUP)
            part = env[:, down, rows, :].reshape(wide, block)
            made = dot(mix_high, part) + dot(mix_low, part)
            mixed[:, down, rows, :] = made.astype(BF16).reshape(channels, GROUP, block)


def first_images(
    lists_held,
    sizes_held,
    left_a,
    right_a,
    left_b,
    right_b,
    starts,
    swapped,
    shifted,
    own_images,
    rest,
    sent,
    halo_images,
    row,
    halo,
    lists,
    sizes,
    sems,
):
    lists_copy = pltpu.make_async_copy(lists_held, lists, sems.at[0])
    lists_copy.start()
    sizes_copy = pltpu.make_async_copy(sizes_held, sizes, sems.at[1])
    sizes_copy.start()
    downs, block = left_a.shape[1], left_a.shape[-1]
    halo_images[...] = jnp.zeros_like(halo_images)
    add_halo_images(
        lists,
        (left_a, left_b),
        (right_a, right_b),
        swapped,
        shifted,
        halo,
        halo_images,
        True,
        lists_copy,
    )
    sizes_copy.wait()
    found = []
    for bond in range(BONDS):
        size = jnp.zeros((1, 1), F32)
        cross = jnp.zeros((1, 1), F32)
        for down in range(downs):
            image = own_images[bond, down] + halo_images[0, bond, down] + halo_images[1, bond, down]
            rest[bond, down] = image
            start = starts[bond, down].astype(F32)
            size += total(start * start)
            cross += total(start * image)
        quotient = jnp.where(size > 0.0, cross / jnp.where(size > 0.0, size, 1.0), 0.0)
        for down in range(downs):
            image = jnp.where(live_of(sizes, bond, down, block), rest[bond, down], 0.0)
            left_over = image - quotient * starts[bond, down].astype(F32)
            rest[bond, down] = left_over
            sent[bond, down] = left_over.astype(BF16)
        offset = bond * BOND_LANES
        found += [(offset + SIZE, size), (offset + QUOTIENT, quotient)]
    row[...] = jnp.broadcast_to(in_lanes(row.shape[1], found), row.shape)


def local_seconds(
    lists,
    left_a,
    right_a,
    left_b,
    right_b,
    sent,
    starts,
    rest,
    own_images,
    halo_images,
    row_in,
    row,
    along,
    sums,
    sems,
):
    downs = left_a.shape[1]
    copies = [
        pltpu.make_async_copy(source.at[BONDS - 1], along.at[index], sems.at[index])
        for index, source in enumerate((starts, sent))
    ]
    for copy in copies:
        copy.start()
    sums[...] = jnp.zeros_like(sums)
    add_local_images(lists, (left_a, left_b), (right_a, right_b), sent, sums)
    found = []
    for bond in range(BONDS):
        numbers = {place: jnp.zeros((1, 1), F32) for place in range(REST, START_HIGH + 1)}
        for down in range(downs):
            start = starts[bond, down].astype(F32)
            left_over = rest[bond, down]
            numbers[REST] += total(left_over * left_over)
            numbers[REST_IMAGE] += total(left_over * sums[bond, down])
            numbers[START_IMAGE] += total(start * sums[bond, down])
            parts = (own_images[bond, down], halo_images[0, bond, down], halo_images[1, bond, down])
            for kind, part in enumerate(parts):
                numbers[REST_OWN + kind] += total(left_over * part)
                numbers[START_OWN + kind] += total(start * part)
        offset = bond * BOND_LANES
        found += [(offset + place, numbers[place]) for place in sorted(numbers)]
    row[...] = row_in[...] + jnp.broadcast_to(in_lanes(row.shape[1], found), row.shape)
    for copy in copies:
        copy.wait()


def halo_seconds(
    lists_held,
    left_a,
    right_a,
    left_b,
    right_b,
    swapped,
    shifted,
    starts,
    rest,
    row_in,
    row,
    halo,
    sums,
    lists,
    lists_sem,
):
    lists_copy = pltpu.make_async_copy(lists_held, lists, lists_sem)
    lists_copy.start()
    downs = left_a.shape[1]
    sums[...] = jnp.zeros_like(sums)
    add_halo_images(
        lists,
        (left_a, left_b),
        (right_a, right_b),
        swapped,
        shifted,
        halo,
        sums,
        False,
        lists_copy,
    )
    found = []
    for bond in range(BONDS):
        of_rest = jnp.zeros((1, 1), F32)
        of_start = jnp.zeros((1, 1), F32)
        for down in range(downs):
            of_rest += total(rest[bond, down] * sums[bond, down])
            of_start += total(starts[bond, down].astype(F32) * sums[bond, down])
        offset = bond * BOND_LANES
        found += [(offset + REST_IMAGE, of_rest), (offset + START_IMAGE, of_start)]
    row[...] = jnp.broadcast_to(row_in[0:1, :] + in_lanes(row.shape[1], found), row.shape)


def ritz(rows):
    ups = rows.shape[1]

    def column(array, place):
        return array[:, :, place : place + 1]

    def over_ups(array):
        return jnp.sum(array, axis=1, keepdims=True)

    size = column(rows, SIZE)
    quotient = column(rows, QUOTIENT)
    norm_sq = over_ups(size)
    alpha_zero = over_ups(size * quotient) / norm_sq
    off = quotient - alpha_zero
    off_low = column(pltpu.roll(rows, 1, 1), QUOTIENT) - alpha_zero
    off_high = column(pltpu.roll(rows, ups - 1, 1), QUOTIENT) - alpha_zero
    residual_sq = over_ups(column(rows, REST) + size * off * off)
    crossed = column(rows, REST_IMAGE) + off * column(rows, START_IMAGE)
    for kind, factor in enumerate((off, off_low, off_high)):
        crossed += factor * (column(rows, REST_OWN + kind) + off * column(rows, START_OWN + kind))
    alpha_one = over_ups(crossed) / residual_sq
    beta_sq = residual_sq / norm_sq
    beta = jnp.sqrt(beta_sq)
    spread = 0.5 * (alpha_zero - alpha_one)
    energy = 0.5 * (alpha_zero + alpha_one) - jnp.sqrt(spread * spread + beta_sq)
    weight_one = energy - alpha_zero
    length = jnp.sqrt(beta_sq + weight_one * weight_one)
    of_rest = weight_one / (beta * length)
    of_start = beta / length + of_rest * off
    return energy, of_start, of_rest


def finish(
    factor,
    ups,
    numbers,
    starts_held,
    rest_held,
    along_held,
    edge_held,
    mixed_held,
    ground_a,
    ground_b,
    energies_out,
    boundary,
    energies,
    starts,
    rest,
    along,
    edge,
    mixed,
    made,
    grounds,
    in_sems,
    mixed_sems,
    out_sems,
):
    channels, downs = mixed.shape[0], mixed.shape[1]

    def arrival(index, source, target):
        copy = pltpu.make_async_copy(source, target, in_sems.at[index])
        copy.start()
        return copy

    first = [
        arrival(0, starts_held.at[0], starts.at[0]),
        arrival(1, rest_held.at[0], rest.at[0]),
        arrival(2, along_held, along),
        arrival(3, edge_held, edge),
    ]
    arrivals = [
        pltpu.make_async_copy(mixed_held.at[index], mixed.at[index], mixed_sems.at[index])
        for index in range(channels)
    ]
    for copy in arrivals[: 2 * BATCH]:
        copy.start()
    second = [
        arrival(4, starts_held.at[1], starts.at[1]),
        arrival(5, rest_held.at[1], rest.at[1]),
    ]
    for copy in arrivals[2 * BATCH :]:
        copy.start()
    segments = numbers.shape[0] // ups
    seg, blk = lax.axis_index("seg"), lax.axis_index("blk")
    here = numbers[pl.ds(pl.multiple_of(seg * ups, ups), ups), :]
    after = jnp.minimum(seg + 1, segments - 1)
    there = numbers[pl.ds(pl.multiple_of(after * ups, ups), ups), :]
    width = numbers.shape[1]
    energy, of_start, of_rest = ritz(
        jnp.stack(
            [
                here,
                pltpu.roll(here, width - BOND_LANES, 1),
                pltpu.roll(there, width - BOND_LANES, 1),
            ]
        )
    )
    place = lax.broadcasted_iota(jnp.int32, of_start.shape, 1)
    of_start = jnp.sum(jnp.where(place == blk, of_start, 0.0), axis=1, keepdims=True)
    lane = lax.broadcasted_iota(jnp.int32, energies.shape, 1)
    energies[...] = jnp.where(lane == 0, energy[0], energy[1])
    last = seg == segments - 1
    out_copies = [pltpu.make_async_copy(energies, energies_out, in_sems.at[6])]
    out_copies[0].start()

    def leave(index, source, target):
        copy = pltpu.make_async_copy(source, target, out_sems.at[index])
        copy.start()
        out_copies.append(copy)

    def ground_of(bond, target):
        for down in range(downs):
            start = starts[bond, down].astype(F32)
            grounds[bond, down] = of_start[bond] * start + of_rest[bond] * rest[bond, down]
        leave(channels + bond, grounds.at[bond], target)

    for copy in first:
        copy.wait()
    products = []
    for down in range(downs):
        start = starts[0, down].astype(F32)
        ground = of_start[0] * start + of_rest[0] * rest[0, down]
        grounds[0, down] = ground
        found = of_start[2] * along[0, down].astype(F32) + of_rest[2] * along[1, down].astype(F32)
        state = jnp.where(last, edge[down], found.astype(BF16))
        product = (dot(ground.astype(BF16), state) * factor).astype(BF16)
        products.append((product, product.T))
    leave(channels, grounds.at[0], ground_a)
    halves = {}

    def last_product(group):
        for channel in group:
            for down, (_, turned) in enumerate(products):
                made[channel, down] = dot(turned, halves[channel, down]).astype(BF16)
        for channel in group:
            leave(channel, made.at[channel], boundary.at[channel])

    groups = [range(i, min(i + BATCH, channels)) for i in range(0, channels, BATCH)]
    for index, group in enumerate(groups):
        for channel in group:
            arrivals[channel].wait()
        for channel in group:
            for down, (product, _) in enumerate(products):
                halves[channel, down] = dot(mixed[channel, down], product).astype(BF16)
        if index > 0:
            last_product(groups[index - 1])
        if index == min(1, len(groups) - 1):
            for copy in second:
                copy.wait()
            ground_of(1, ground_b)
    last_product(groups[-1])
    for copy in out_copies:
        copy.wait()


def swapped_pairs(block):
    devices = range(lax.axis_size("blk"))
    return lax.ppermute(block, "blk", [(i, i ^ 1) for i in devices if i ^ 1 in devices])


def shifted_pairs(block):
    devices = range(lax.axis_size("blk"))
    pairs = [(i, i + 1) for i in devices if i % 2 == 1 and i + 1 in devices]
    return lax.ppermute(block, "blk", pairs + [(j, i) for i, j in pairs])


def from_right_segment(block):
    segments = lax.axis_size("seg")
    return lax.ppermute(block, "seg", [(i + 1, i) for i in range(segments - 1)])


def local(
    guess_a,
    guess_b,
    left_env_a,
    right_env_a,
    left_env_b,
    right_env_b,
    channel_mix,
    term_shift,
    sector_sizes,
    edge_state,
):
    block = guess_a.shape[-1]
    downs = guess_a.shape[2]
    channels = left_env_a.shape[1]
    ups = lax.axis_size("blk")
    devices = ups * lax.axis_size("seg")
    pair = (downs, block, block)
    both = (BONDS,) + pair
    env_shape = (channels, downs, block, block)
    held = [in_hbm(env.reshape(env_shape)) for env in (left_env_a, right_env_a, left_env_b, right_env_b)]
    bits = 2 * downs * block * block
    env_bytes = channels * bits
    apply_flops = 4 * channels * downs * block**3
    sizes = in_hbm(sector_sizes.transpose(0, 2, 3, 1))
    tile = jax.ShapeDtypeStruct((8, 128), F32)

    (starts,) = call(
        masked_starts,
        "masked_starts",
        [HBM, HBM, HBM],
        [(VMEM, pltpu.VMEM(both, BF16))],
        [pltpu.SMEM(sizes.shape, jnp.int32), pltpu.SemaphoreType.DMA(()), pltpu.SemaphoreType.DMA((BONDS, downs))],
        4 * downs * block * block,
        4 * bits,
    )(sizes, in_hbm(guess_a.reshape(pair)), in_hbm(guess_b.reshape(pair)))
    shifted, swapped = shifted_pairs(starts), swapped_pairs(starts)

    *loaded, own_images, lists = call(
        opening,
        "opening",
        [SMEM, VMEM] + [HBM] * 4,
        [(VMEM, pltpu.VMEM(env_shape, BF16))] * 4
        + [
            (VMEM, pltpu.VMEM(both, F32)),
            (SMEM, jax.ShapeDtypeStruct((CODES + 2, channels + 1), jnp.int32)),
        ],
        [pltpu.SemaphoreType.DMA((channels,))],
        apply_flops,
        5 * env_bytes,
    )(in_hbm(term_shift), starts, *held)

    halo = pltpu.VMEM((2,) + both, BF16)
    rest, sent, halo_images, row = call(
        first_images,
        "first_images",
        [VMEM, HBM] + [VMEM] * 8,
        [
            (VMEM, pltpu.VMEM(both, F32)),
            (VMEM, pltpu.VMEM(both, BF16)),
            (VMEM, pltpu.VMEM((2,) + both, F32)),
            (VMEM, tile),
        ],
        [
            halo,
            pltpu.SMEM(lists.shape, jnp.int32),
            pltpu.SMEM(sizes.shape, jnp.int32),
            pltpu.SemaphoreType.DMA((2,)),
        ],
        apply_flops,
        env_bytes,
    )(lists, sizes, *loaded, starts, swapped, shifted, own_images)
    shifted, swapped = shifted_pairs(sent), swapped_pairs(sent)
    row, along = call(
        local_seconds,
        "local_seconds",
        [SMEM] + [VMEM] * 10,
        [(VMEM, tile), (HBM, jax.ShapeDtypeStruct((2,) + pair, BF16))],
        [pltpu.VMEM(both, F32), pltpu.SemaphoreType.DMA((2,))],
        apply_flops,
        env_bytes,
    )(lists, *loaded, sent, starts, rest, own_images, halo_images, row)
    from_next = from_right_segment(along)
    (row,) = call(
        halo_seconds,
        "halo_seconds",
        [VMEM] + [VMEM] * 9,
        [(VMEM, pltpu.VMEM((devices, 128), F32))],
        [
            halo,
            pltpu.VMEM(both, F32),
            pltpu.SMEM(lists.shape, jnp.int32),
            pltpu.SemaphoreType.DMA(()),
        ],
        apply_flops,
        env_bytes,
    )(lists, *loaded, swapped, shifted, starts, rest, row)
    numbers = lax.all_to_all(row, ("seg", "blk"), 0, 0, tiled=True)
    (mixed,) = call(
        mixing,
        "mixing",
        [VMEM, VMEM, HBM],
        [(VMEM, jax.ShapeDtypeStruct(env_shape, BF16))],
        [],
        4 * channels * channels * GROUP * downs * block * block,
        2 * env_bytes,
    )(channel_mix, loaded[0], row)
    state32 = jax.ShapeDtypeStruct(pair, F32)
    ground_a, ground_b, energies, boundary = call(
        functools.partial(finish, 1.0 / block, ups),
        "finish",
        [VMEM] + [HBM] * 5,
        [
            (HBM, state32),
            (HBM, state32),
            (HBM, jax.ShapeDtypeStruct((1, 2), F32)),
            (HBM, jax.ShapeDtypeStruct(env_shape, BF16)),
        ],
        [
            pltpu.VMEM((1, 2), F32),
            pltpu.VMEM(both, BF16),
            pltpu.VMEM(both, F32),
            pltpu.VMEM((2,) + pair, BF16),
            pltpu.VMEM(pair, BF16),
            pltpu.VMEM(env_shape, BF16),
            pltpu.VMEM(env_shape, BF16),
            pltpu.VMEM(both, F32),
            pltpu.SemaphoreType.DMA((7,)),
            pltpu.SemaphoreType.DMA((channels,)),
            pltpu.SemaphoreType.DMA((channels + BONDS,)),
        ],
        apply_flops,
        2 * env_bytes,
    )(
        numbers,
        *(in_hbm(x) for x in (starts, rest, from_next, edge_state.reshape(pair), mixed)),
    )
    return (
        ground_a.reshape(guess_a.shape),
        ground_b.reshape(guess_b.shape),
        energies,
        boundary.reshape(left_env_a.shape),
    )


def solution(mesh):
    placed = (
        P("seg", "blk", None, None, None),
        P("seg", "blk", None, None, None),
        P("seg", None, "blk", None, None, None),
        P("seg", None, "blk", None, None, None),
        P("seg", None, "blk", None, None, None),
        P("seg", None, "blk", None, None, None),
        P(),
        P(),
        P("seg", None, "blk", None),
        P("blk", None, None, None),
    )
    return jax.shard_map(
        local,
        mesh=mesh,
        in_specs=placed,
        out_specs=(
            P("seg", "blk", None, None, None),
            P("seg", "blk", None, None, None),
            P("seg", None),
            P("seg", None, "blk", None, None, None),
        ),
        check_vma=False,
    )
```

```python
import functools

import jax
import jax.numpy as jnp
from jax import lax
from jax.experimental import pallas as pl
from jax.experimental.pallas import tpu as pltpu
from jax.sharding import PartitionSpec as P

F32 = jnp.float32
BF16 = jnp.bfloat16
VMEM = pl.BlockSpec(memory_space=pltpu.VMEM)
SMEM = pl.BlockSpec(memory_space=pltpu.SMEM)
HBM = pl.BlockSpec(memory_space=pltpu.HBM)
MIB = 1 << 20
GROUP = 16
BATCH = 4
BONDS = 2

CHANNEL, KIND, DOWN, SOURCE, OPENS = range(5)
EARLY, LATE = 0, OPENS + 1
LIST_ROWS = LATE + SOURCE + 1


(
    SIZE,
    QUOTIENT,
    REST,
    REST_IMAGE,
    START_IMAGE,
    REST_OWN,
    REST_SWAPPED,
    START_OWN,
    START_SWAPPED,
) = range(9)
BOND_LANES = 64


def call(body, name, ins, outs, scratch, flops, moved, limit=20 * MIB):
    return pl.pallas_call(
        body,
        name=name,
        in_specs=ins,
        out_specs=tuple(spec for spec, _ in outs),
        out_shape=tuple(shape for _, shape in outs),
        scratch_shapes=scratch,
        cost_estimate=pl.CostEstimate(flops=flops, bytes_accessed=moved, transcendentals=0),
        compiler_params=pltpu.CompilerParams(vmem_limit_bytes=limit),
    )


def in_hbm(array):
    return pltpu.with_memory_space_constraint(array, pltpu.HBM)


def live(rows, cols, block):
    row = lax.broadcasted_iota(jnp.int32, (block, block), 0)
    col = lax.broadcasted_iota(jnp.int32, (block, block), 1)
    return (row < rows) & (col < cols)


def live_of(sizes, bond, down, block):
    return live(sizes[0, 0, down, 2 * bond], sizes[0, 0, down, 2 * bond + 1], block)


def dot(left, right):
    return jnp.dot(left, right, preferred_element_type=F32)


def dot_by_rows(left, right):
    return lax.dot_general(left, right, (((1,), (1,)), ((), ())), preferred_element_type=F32)


def exact_dot(left, right):
    return jnp.dot(left, right, precision=lax.Precision.HIGHEST, preferred_element_type=F32)


def total(array):
    return jnp.sum(jnp.sum(array, axis=0, keepdims=True), axis=1, keepdims=True)


def in_lanes(width, pairs):
    lane = lax.broadcasted_iota(jnp.int32, (1, width), 1)
    row = jnp.zeros((1, width), F32)
    for place, value in pairs:
        row = jnp.where(lane == place, value, row)
    return row


def masked_starts(sizes_held, guess_a, guess_b, starts, sizes, size_sem, sems):
    sizes_copy = pltpu.make_async_copy(sizes_held, sizes, size_sem)
    sizes_copy.start()
    downs, block = starts.shape[1], starts.shape[-1]
    places = [(bond, down) for bond in range(BONDS) for down in range(downs)]
    copies = [
        pltpu.make_async_copy(
            (guess_a, guess_b)[bond].at[down], starts.at[bond, down], sems.at[bond, down]
        )
        for bond, down in places
    ]
    for copy in copies:
        copy.start()
    sizes_copy.wait()
    for copy, (bond, down) in zip(copies, places):
        copy.wait()
        start = starts[bond, down]
        starts[bond, down] = jnp.where(
            live_of(sizes, bond, down, block), start, jnp.zeros_like(start)
        )


def is_late(code):
    even = lax.rem(lax.axis_index("blk"), 2) == 0
    return code == jnp.where(even, 1, 2)


def list_units(shift, downs, lists):
    channels = shift.shape[0]
    end = channels * downs
    early, late = jnp.int32(0), jnp.int32(0)
    for channel in range(channels):
        code = shift[channel]
        far = is_late(code)
        near = jnp.logical_not(far) & ((code == 1) | (code == 2))
        move = (code == 4).astype(jnp.int32) - (code == 3).astype(jnp.int32)
        opens = jnp.int32(1)
        for down in range(downs):
            source = down + move
            here = jnp.logical_not(far) & (source >= 0) & (source < downs)
            lists[EARLY + CHANNEL, early] = jnp.int32(channel)
            lists[EARLY + KIND, early] = near.astype(jnp.int32)
            lists[EARLY + DOWN, early] = jnp.int32(down)
            lists[EARLY + SOURCE, early] = jnp.where(near, downs + down, source)
            lists[EARLY + OPENS, early] = opens
            lists[LATE + CHANNEL, late] = jnp.int32(channel)
            lists[LATE + KIND, late] = jnp.int32(0)
            lists[LATE + DOWN, late] = jnp.int32(down)
            lists[LATE + SOURCE, late] = jnp.int32(down)
            opens = jnp.where(here, 0, opens)
            early = early + here.astype(jnp.int32)
            late = late + far.astype(jnp.int32)
    lists[EARLY, end] = early
    lists[LATE, end] = late


class Unparted:
    def __init__(self, sums):
        self.sums = sums

    def __getitem__(self, place):
        return self.sums[place[1:]]

    def __setitem__(self, place, value):
        self.sums[place[1:]] = value


def add_units(lists, base, lefts, rights, sources, sums, arrived=None):
    def images(indices):
        units = [
            [lists[base + part, index] for part in (CHANNEL, KIND, DOWN, SOURCE)]
            for index in indices
        ]
        if arrived is not None:
            for index, unit in zip(indices, units):
                pl.when(lists[base + OPENS, index] == 1)(functools.partial(arrived, unit[0]))
        halves = [
            [
                dot(lefts[bond][channel, down], sources[bond, source]).astype(BF16)
                for bond in range(BONDS)
            ]
            for channel, _, down, source in units
        ]
        for (channel, kind, down, _), half in zip(units, halves):
            for bond in range(BONDS):
                sums[kind, bond, down] += dot_by_rows(half[bond], rights[bond][channel, down])

    count = lists[base, lists.shape[1] - 1]
    done = jnp.int32(0)
    for size in (4, 2, 1):
        steps = lax.div(count - done, size)

        def step(index, carry, size=size, done=done):
            first = done + size * index
            images([first + i for i in range(size)])
            return carry

        lax.fori_loop(0, steps, step, 0)
        done = done + size * steps


def fill_sources(own, swapped, sources):
    downs = own.shape[1]
    for bond in range(BONDS):
        for down in range(downs):
            sources[bond, down] = own[bond, down]
            sources[bond, downs + down] = swapped[bond, down]


def opening(shift, starts, swapped, *refs):
    held, loaded, (images, row, lists, sources, sems) = refs[:4], refs[4:8], refs[8:]
    left_a, right_a, left_b, right_b = loaded
    channels, downs = left_a.shape[0], left_a.shape[1]

    def copies(channel):
        return [
            pltpu.make_async_copy(source.at[channel], target.at[channel], sems.at[channel])
            for source, target in zip(held, loaded)
        ]

    def bring(channel):
        for copy in copies(channel):
            copy.start()

    def await_one(channel):
        for copy in copies(channel):
            copy.wait()

    for channel in range(channels):
        pl.when(jnp.logical_not(is_late(shift[channel])))(functools.partial(bring, channel))
    for channel in range(channels):
        pl.when(is_late(shift[channel]))(functools.partial(bring, channel))
    list_units(shift, downs, lists)
    images[...] = jnp.zeros_like(images)
    fill_sources(starts, swapped, sources)
    found = []
    for bond in range(BONDS):
        size = jnp.zeros((1, 1), F32)
        for down in range(downs):
            start = starts[bond, down].astype(F32)
            size += total(start * start)
        found.append((bond * BOND_LANES + SIZE, size))
    add_units(lists, EARLY, (left_a, left_b), (right_a, right_b), sources, images, await_one)
    for bond in range(BONDS):
        numbers = [jnp.zeros((1, 1), F32) for _ in range(2)]
        for down in range(downs):
            start = starts[bond, down].astype(F32)
            for kind in range(2):
                numbers[kind] += total(start * images[kind, bond, down])
        found += [(bond * BOND_LANES + START_OWN + kind, numbers[kind]) for kind in range(2)]
    row[...] = jnp.broadcast_to(in_lanes(row.shape[1], found), row.shape)
    for channel in range(channels):
        pl.when(is_late(shift[channel]))(functools.partial(await_one, channel))


def mixing(mix, env, after, mixed):
    del after
    channels, downs, block = env.shape[0], env.shape[1], env.shape[-1]
    wide = channels * GROUP
    squared = exact_dot(mix[...], mix[...])
    spread_rows = (
        lax.broadcasted_iota(jnp.int32, (wide, channels), 0) // GROUP
        == lax.broadcasted_iota(jnp.int32, (wide, channels), 1)
    ).astype(F32)
    spread_cols = (
        lax.broadcasted_iota(jnp.int32, (channels, wide), 1) // GROUP
        == lax.broadcasted_iota(jnp.int32, (channels, wide), 0)
    ).astype(F32)
    spread = exact_dot(exact_dot(spread_rows, squared), spread_cols)
    same = lax.rem(lax.broadcasted_iota(jnp.int32, (wide, wide), 0), GROUP) == lax.rem(
        lax.broadcasted_iota(jnp.int32, (wide, wide), 1), GROUP
    )
    spread = jnp.where(same, spread, 0.0)
    mix_high = spread.astype(BF16)
    mix_low = (spread - mix_high.astype(F32)).astype(BF16)
    for down in range(downs):
        for group in range(block // GROUP):
            rows = slice(group * GROUP, (group + 1) * GROUP)
            part = env[:, down, rows, :].reshape(wide, block)
            made = dot(mix_high, part) + dot(mix_low, part)
            mixed[:, down, rows, :] = made.astype(BF16).reshape(channels, GROUP, block)


def first_images(
    lists_held,
    sizes_held,
    left_a,
    right_a,
    left_b,
    right_b,
    starts,
    shifted,
    images,
    row_in,
    rest,
    sent,
    row,
    late,
    lists,
    sizes,
    sems,
):
    lists_copy = pltpu.make_async_copy(lists_held, lists, sems.at[0])
    lists_copy.start()
    sizes_copy = pltpu.make_async_copy(sizes_held, sizes, sems.at[1])
    sizes_copy.start()
    downs, block = left_a.shape[1], left_a.shape[-1]
    late[...] = jnp.zeros_like(late)
    lists_copy.wait()
    add_units(lists, LATE, (left_a, left_b), (right_a, right_b), shifted, late)
    sizes_copy.wait()
    found = []
    for bond in range(BONDS):
        at = bond * BOND_LANES + SIZE
        size = row_in[0:1, at : at + 1]
        cross = jnp.zeros((1, 1), F32)
        for down in range(downs):
            image = images[0, bond, down] + images[1, bond, down] + late[0, bond, down]
            rest[bond, down] = image
            cross += total(starts[bond, down].astype(F32) * image)
        quotient = jnp.where(size > 0.0, cross / jnp.where(size > 0.0, size, 1.0), 0.0)
        for down in range(downs):
            image = jnp.where(live_of(sizes, bond, down, block), rest[bond, down], 0.0)
            left_over = image - quotient * starts[bond, down].astype(F32)
            rest[bond, down] = left_over
            sent[bond, down] = left_over.astype(BF16)
        found.append((bond * BOND_LANES + QUOTIENT, quotient))
    row[...] = row_in[...] + jnp.broadcast_to(in_lanes(row.shape[1], found), row.shape)


def early_seconds(
    lists_held,
    left_a,
    right_a,
    left_b,
    right_b,
    sent,
    swapped,
    starts,
    rest,
    images,
    row_in,
    row,
    sums,
    along,
    sources,
    lists,
    lists_sem,
    sems,
):
    lists_copy = pltpu.make_async_copy(lists_held, lists, lists_sem)
    lists_copy.start()
    downs = left_a.shape[1]
    copies = [
        pltpu.make_async_copy(source.at[BONDS - 1], along.at[index], sems.at[index])
        for index, source in enumerate((starts, sent))
    ]
    for copy in copies:
        copy.start()
    sums[...] = jnp.zeros_like(sums)
    fill_sources(sent, swapped, sources)
    lists_copy.wait()
    add_units(lists, EARLY, (left_a, left_b), (right_a, right_b), sources, Unparted(sums))
    found = []
    for bond in range(BONDS):
        numbers = {place: jnp.zeros((1, 1), F32) for place in (REST, REST_OWN, REST_SWAPPED)}
        for down in range(downs):
            left_over = rest[bond, down]
            numbers[REST] += total(left_over * left_over)
            for kind in range(2):
                numbers[REST_OWN + kind] += total(left_over * images[kind, bond, down])
        offset = bond * BOND_LANES
        found += [(offset + place, numbers[place]) for place in sorted(numbers)]
    row[...] = row_in[...] + jnp.broadcast_to(in_lanes(row.shape[1], found), row.shape)
    for copy in copies:
        copy.wait()


def late_seconds(
    lists_held,
    left_a,
    right_a,
    left_b,
    right_b,
    shifted,
    starts,
    rest,
    early_sums,
    row_in,
    row,
    sums,
    lists,
    lists_sem,
):
    lists_copy = pltpu.make_async_copy(lists_held, lists, lists_sem)
    lists_copy.start()
    downs = left_a.shape[1]
    sums[...] = early_sums[...]
    lists_copy.wait()
    add_units(lists, LATE, (left_a, left_b), (right_a, right_b), shifted, Unparted(sums))
    found = []
    for bond in range(BONDS):
        of_rest = jnp.zeros((1, 1), F32)
        of_start = jnp.zeros((1, 1), F32)
        for down in range(downs):
            of_rest += total(rest[bond, down] * sums[bond, down])
            of_start += total(starts[bond, down].astype(F32) * sums[bond, down])
        offset = bond * BOND_LANES
        found += [(offset + REST_IMAGE, of_rest), (offset + START_IMAGE, of_start)]
    row[...] = jnp.broadcast_to(row_in[0:1, :] + in_lanes(row.shape[1], found), row.shape)


def ritz(numbers, bond, first, ups, place):
    lane = lax.broadcasted_iota(jnp.int32, (1, numbers.shape[1]), 1)
    inside = (lane >= first) & (lane < first + ups)

    def part(index):
        at = bond * BOND_LANES + index
        return numbers[at : at + 1]

    def over_ups(values):
        return jnp.sum(jnp.where(inside, values, 0.0), axis=1, keepdims=True)

    size = part(SIZE)
    quotient = part(QUOTIENT)
    low = pltpu.roll(quotient, 1, 1)
    high = pltpu.roll(quotient, quotient.shape[1] - 1, 1)
    even = (lane & 1) == 0
    none_low, none_high = lane == first, lane == first + ups - 1
    norm_sq = over_ups(size)
    alpha_zero = over_ups(size * quotient) / norm_sq
    off = quotient - alpha_zero
    off_low = jnp.where(none_low, 0.0, low - alpha_zero)
    off_high = jnp.where(none_high, 0.0, high - alpha_zero)
    off_swapped = jnp.where(even, off_high, off_low)
    off_shifted = jnp.where(even, off_low, off_high)
    residual_sq = over_ups(part(REST) + size * off * off)
    crossed = part(REST_IMAGE) + off * part(START_IMAGE)
    rest_of = [part(REST_OWN), part(REST_SWAPPED)]
    start_of = [part(START_OWN), part(START_SWAPPED)]
    rest_of.append(part(REST) - rest_of[0] - rest_of[1])
    start_of.append(quotient * size - start_of[0] - start_of[1])
    for factor, of_rest, of_start in zip((off, off_swapped, off_shifted), rest_of, start_of):
        crossed += factor * (of_rest + off * of_start)
    alpha_one = over_ups(crossed) / residual_sq
    beta_sq = residual_sq / norm_sq
    beta = jnp.sqrt(beta_sq)
    spread = 0.5 * (alpha_zero - alpha_one)
    energy = 0.5 * (alpha_zero + alpha_one) - jnp.sqrt(spread * spread + beta_sq)
    weight_one = energy - alpha_zero
    length = jnp.sqrt(beta_sq + weight_one * weight_one)
    of_rest = weight_one / (beta * length)
    own_off = jnp.sum(jnp.where(lane == first + place, off, 0.0), axis=1, keepdims=True)
    return energy, beta / length + of_rest * own_off, of_rest


def finish(
    factor,
    ups,
    numbers,
    starts_held,
    rest_held,
    along_held,
    edge_held,
    mixed_held,
    ground_a,
    ground_b,
    energies_out,
    boundary,
    energies,
    starts,
    rest,
    along,
    edge,
    mixed,
    made,
    grounds,
    in_sems,
    mixed_sems,
    out_sems,
):
    channels, downs = mixed.shape[0], mixed.shape[1]

    def arrival(index, source, target):
        copy = pltpu.make_async_copy(source, target, in_sems.at[index])
        copy.start()
        return copy

    first = [
        arrival(0, starts_held.at[0], starts.at[0]),
        arrival(1, rest_held.at[0], rest.at[0]),
        arrival(2, along_held, along),
        arrival(3, edge_held, edge),
    ]
    arrivals = [
        pltpu.make_async_copy(mixed_held.at[index], mixed.at[index], mixed_sems.at[index])
        for index in range(channels)
    ]
    for copy in arrivals[: 2 * BATCH]:
        copy.start()
    second = [
        arrival(4, starts_held.at[1], starts.at[1]),
        arrival(5, rest_held.at[1], rest.at[1]),
    ]
    for copy in arrivals[2 * BATCH :]:
        copy.start()
    devices, width = numbers.shape
    segments = devices // ups
    seg, blk = lax.axis_index("seg"), lax.axis_index("blk")
    after = jnp.minimum(seg + 1, segments - 1)
    padding = [jnp.zeros((-devices % width, width), F32)] if devices % width else []
    by_place = jnp.concatenate([numbers[...], *padding]).T
    solves = [
        ritz(by_place, bond, at * ups, ups, blk) for bond, at in ((0, seg), (1, seg), (1, after))
    ]
    energy, of_start, of_rest = zip(*solves)
    lane = lax.broadcasted_iota(jnp.int32, energies.shape, 1)
    energies[...] = jnp.where(lane == 0, energy[0], energy[1])
    last = seg == segments - 1
    out_copies = [pltpu.make_async_copy(energies, energies_out, in_sems.at[6])]
    out_copies[0].start()

    def leave(index, source, target):
        copy = pltpu.make_async_copy(source, target, out_sems.at[index])
        copy.start()
        out_copies.append(copy)

    def ground_of(bond, target):
        for down in range(downs):
            start = starts[bond, down].astype(F32)
            grounds[bond, down] = of_start[bond] * start + of_rest[bond] * rest[bond, down]
        leave(channels + bond, grounds.at[bond], target)

    for copy in first:
        copy.wait()
    products = []
    for down in range(downs):
        start = starts[0, down].astype(F32)
        ground = of_start[0] * start + of_rest[0] * rest[0, down]
        grounds[0, down] = ground
        found = of_start[2] * along[0, down].astype(F32) + of_rest[2] * along[1, down].astype(F32)
        state = jnp.where(last, edge[down], found.astype(BF16))
        product = (dot(ground.astype(BF16), state) * factor).astype(BF16)
        products.append((product, product.T))
    leave(channels, grounds.at[0], ground_a)
    halves = {}

    def last_product(group):
        for channel in group:
            for down, (_, turned) in enumerate(products):
                made[channel, down] = dot(turned, halves[channel, down]).astype(BF16)
        for channel in group:
            leave(channel, made.at[channel], boundary.at[channel])

    groups = []
    while sum(map(len, groups)) < channels:
        at = sum(map(len, groups))
        groups.append(range(at, at + min(BATCH, (channels - at + 1) // 2)))
    for index, group in enumerate(groups):
        for channel in group:
            arrivals[channel].wait()
        for down, (product, _) in enumerate(products):
            block = product.shape[0]
            stacked = mixed[group.start : group.stop, down].reshape(len(group) * block, block)
            half = dot(stacked, product).astype(BF16)
            for place, channel in enumerate(group):
                halves[channel, down] = half[place * block : (place + 1) * block]
        if index > 0:
            last_product(groups[index - 1])
        if index == min(1, len(groups) - 1):
            for copy in second:
                copy.wait()
            ground_of(1, ground_b)
    last_product(groups[-1])
    for copy in out_copies:
        copy.wait()


def swapped_pairs(block):
    devices = range(lax.axis_size("blk"))
    return lax.ppermute(block, "blk", [(i, i ^ 1) for i in devices if i ^ 1 in devices])


def shifted_pairs(block):
    devices = range(lax.axis_size("blk"))
    pairs = [(i, i + 1) for i in devices if i % 2 == 1 and i + 1 in devices]
    return lax.ppermute(block, "blk", pairs + [(j, i) for i, j in pairs])


def from_right_segment(block):
    segments = lax.axis_size("seg")
    return lax.ppermute(block, "seg", [(i + 1, i) for i in range(segments - 1)])


def local(
    guess_a,
    guess_b,
    left_env_a,
    right_env_a,
    left_env_b,
    right_env_b,
    channel_mix,
    term_shift,
    sector_sizes,
    edge_state,
):
    block = guess_a.shape[-1]
    downs = guess_a.shape[2]
    channels = left_env_a.shape[1]
    ups = lax.axis_size("blk")
    devices = ups * lax.axis_size("seg")
    pair = (downs, block, block)
    both = (BONDS,) + pair
    env_shape = (channels, downs, block, block)
    held = [in_hbm(env.reshape(env_shape)) for env in (left_env_a, right_env_a, left_env_b, right_env_b)]
    bits = 2 * downs * block * block
    env_bytes = channels * bits
    apply_flops = 4 * channels * downs * block**3
    sizes = in_hbm(sector_sizes.transpose(0, 2, 3, 1))
    tile = jax.ShapeDtypeStruct((8, 128), F32)

    (starts,) = call(
        masked_starts,
        "masked_starts",
        [HBM, HBM, HBM],
        [(VMEM, pltpu.VMEM(both, BF16))],
        [pltpu.SMEM(sizes.shape, jnp.int32), pltpu.SemaphoreType.DMA(()), pltpu.SemaphoreType.DMA((BONDS, downs))],
        4 * downs * block * block,
        4 * bits,
    )(sizes, in_hbm(guess_a.reshape(pair)), in_hbm(guess_b.reshape(pair)))
    swapped, shifted = swapped_pairs(starts), shifted_pairs(starts)

    list_shape = (LIST_ROWS, channels * downs + 1)
    sources = pltpu.VMEM((BONDS, 2 * downs, block, block), BF16)
    *loaded, images, row, lists = call(
        opening,
        "opening",
        [SMEM, VMEM, VMEM] + [HBM] * 4,
        [(VMEM, pltpu.VMEM(env_shape, BF16))] * 4
        + [
            (VMEM, pltpu.VMEM((2,) + both, F32)),
            (VMEM, tile),
            (SMEM, jax.ShapeDtypeStruct(list_shape, jnp.int32)),
        ],
        [sources, pltpu.SemaphoreType.DMA((channels,))],
        apply_flops,
        5 * env_bytes,
    )(in_hbm(term_shift), starts, swapped, *held)

    rest, sent, row = call(
        first_images,
        "first_images",
        [VMEM, HBM] + [VMEM] * 8,
        [
            (VMEM, pltpu.VMEM(both, F32)),
            (VMEM, pltpu.VMEM(both, BF16)),
            (VMEM, tile),
        ],
        [
            pltpu.VMEM((1,) + both, F32),
            pltpu.SMEM(list_shape, jnp.int32),
            pltpu.SMEM(sizes.shape, jnp.int32),
            pltpu.SemaphoreType.DMA((2,)),
        ],
        apply_flops,
        env_bytes,
    )(lists, sizes, *loaded, starts, shifted, images, row)
    swapped, shifted = swapped_pairs(sent), shifted_pairs(sent)
    row, sums, along = call(
        early_seconds,
        "early_seconds",
        [VMEM] * 11,
        [
            (VMEM, tile),
            (VMEM, pltpu.VMEM(both, F32)),
            (HBM, jax.ShapeDtypeStruct((2,) + pair, BF16)),
        ],
        [
            sources,
            pltpu.SMEM(list_shape, jnp.int32),
            pltpu.SemaphoreType.DMA(()),
            pltpu.SemaphoreType.DMA((2,)),
        ],
        apply_flops,
        env_bytes,
    )(lists, *loaded, sent, swapped, starts, rest, images, row)
    from_next = from_right_segment(along)
    (row,) = call(
        late_seconds,
        "late_seconds",
        [VMEM] * 10,
        [(VMEM, pltpu.VMEM((devices, 128), F32))],
        [
            pltpu.VMEM(both, F32),
            pltpu.SMEM(list_shape, jnp.int32),
            pltpu.SemaphoreType.DMA(()),
        ],
        apply_flops,
        env_bytes,
    )(lists, *loaded, shifted, starts, rest, sums, row)
    numbers = lax.all_to_all(row, ("seg", "blk"), 0, 0, tiled=True)
    (mixed,) = call(
        mixing,
        "mixing",
        [VMEM, VMEM, HBM],
        [(VMEM, jax.ShapeDtypeStruct(env_shape, BF16))],
        [],
        4 * channels * channels * GROUP * downs * block * block,
        2 * env_bytes,
    )(channel_mix, loaded[0], row)
    state32 = jax.ShapeDtypeStruct(pair, F32)
    ground_a, ground_b, energies, boundary = call(
        functools.partial(finish, 1.0 / block, ups),
        "finish",
        [VMEM] + [HBM] * 5,
        [
            (HBM, state32),
            (HBM, state32),
            (HBM, jax.ShapeDtypeStruct((1, 2), F32)),
            (HBM, jax.ShapeDtypeStruct(env_shape, BF16)),
        ],
        [
            pltpu.VMEM((1, 2), F32),
            pltpu.VMEM(both, BF16),
            pltpu.VMEM(both, F32),
            pltpu.VMEM((2,) + pair, BF16),
            pltpu.VMEM(pair, BF16),
            pltpu.VMEM(env_shape, BF16),
            pltpu.VMEM(env_shape, BF16),
            pltpu.VMEM(both, F32),
            pltpu.SemaphoreType.DMA((7,)),
            pltpu.SemaphoreType.DMA((channels,)),
            pltpu.SemaphoreType.DMA((channels + BONDS,)),
        ],
        apply_flops,
        2 * env_bytes,
    )(
        numbers,
        *(in_hbm(x) for x in (starts, rest, from_next, edge_state.reshape(pair), mixed)),
    )
    return (
        ground_a.reshape(guess_a.shape),
        ground_b.reshape(guess_b.shape),
        energies,
        boundary.reshape(left_env_a.shape),
    )


def solution(mesh):
    placed = (
        P("seg", "blk", None, None, None),
        P("seg", "blk", None, None, None),
        P("seg", None, "blk", None, None, None),
        P("seg", None, "blk", None, None, None),
        P("seg", None, "blk", None, None, None),
        P("seg", None, "blk", None, None, None),
        P(),
        P(),
        P("seg", None, "blk", None),
        P("blk", None, None, None),
    )
    return jax.shard_map(
        local,
        mesh=mesh,
        in_specs=placed,
        out_specs=(
            P("seg", "blk", None, None, None),
            P("seg", "blk", None, None, None),
            P("seg", None),
            P("seg", None, "blk", None, None, None),
        ),
        check_vma=False,
    )
```

```python
import functools

import jax
import jax.numpy as jnp
from jax import lax
from jax.experimental import pallas as pl
from jax.experimental.pallas import tpu as pltpu
from jax.sharding import PartitionSpec as P

F32 = jnp.float32
BF16 = jnp.bfloat16
VMEM = pl.BlockSpec(memory_space=pltpu.VMEM)
SMEM = pl.BlockSpec(memory_space=pltpu.SMEM)
HBM = pl.BlockSpec(memory_space=pltpu.HBM)
MIB = 1 << 20
GROUP = 16
BATCH = 6
BONDS = 2

CHANNEL, KIND, DOWN, SOURCE, OPENS = range(5)
EARLY, LATE = 0, OPENS + 1
LIST_ROWS = LATE + SOURCE + 1


(
    SIZE,
    QUOTIENT,
    REST,
    START_REST,
    REST_IMAGE,
    START_IMAGE,
    REST_OWN,
    REST_SWAPPED,
    START_OWN,
    START_SWAPPED,
) = range(10)
BOND_LANES = 64


def call(body, name, ins, outs, scratch, flops, moved, limit=20 * MIB):
    return pl.pallas_call(
        body,
        name=name,
        in_specs=ins,
        out_specs=tuple(spec for spec, _ in outs),
        out_shape=tuple(shape for _, shape in outs),
        scratch_shapes=scratch,
        cost_estimate=pl.CostEstimate(flops=flops, bytes_accessed=moved, transcendentals=0),
        compiler_params=pltpu.CompilerParams(vmem_limit_bytes=limit),
    )


def in_hbm(array):
    return pltpu.with_memory_space_constraint(array, pltpu.HBM)


def live(rows, cols, block):
    row = lax.broadcasted_iota(jnp.int32, (block, block), 0)
    col = lax.broadcasted_iota(jnp.int32, (block, block), 1)
    return (row < rows) & (col < cols)


def live_of(sizes, bond, down, block):
    return live(sizes[0, 0, down, 2 * bond], sizes[0, 0, down, 2 * bond + 1], block)


def dot(left, right):
    return jnp.dot(left, right, preferred_element_type=F32)


def dot_by_rows(left, right):
    return lax.dot_general(left, right, (((1,), (1,)), ((), ())), preferred_element_type=F32)


def exact_dot(left, right):
    return jnp.dot(left, right, precision=lax.Precision.HIGHEST, preferred_element_type=F32)


def total(array):
    return jnp.sum(jnp.sum(array, axis=0, keepdims=True), axis=1, keepdims=True)


def folded(array):
    return jnp.sum(array.reshape(-1, 8, array.shape[-1]), axis=0)


def totals(parts):
    rows = parts[0].shape[0]
    by_row = jnp.sum(jnp.concatenate(parts), axis=1, keepdims=True)
    return [
        jnp.sum(by_row[i * rows : (i + 1) * rows], axis=0, keepdims=True) for i in range(len(parts))
    ]


def in_lanes(width, pairs):
    lane = lax.broadcasted_iota(jnp.int32, (1, width), 1)
    row = jnp.zeros((1, width), F32)
    for place, value in pairs:
        row = jnp.where(lane == place, value, row)
    return row


def masked_starts(sizes_held, guess_a, guess_b, starts, sizes, size_sem, sems):
    sizes_copy = pltpu.make_async_copy(sizes_held, sizes, size_sem)
    sizes_copy.start()
    downs, block = starts.shape[1], starts.shape[-1]
    places = [(bond, down) for bond in range(BONDS) for down in range(downs)]
    copies = [
        pltpu.make_async_copy(
            (guess_a, guess_b)[bond].at[down], starts.at[bond, down], sems.at[bond, down]
        )
        for bond, down in places
    ]
    for copy in copies:
        copy.start()
    sizes_copy.wait()
    for copy, (bond, down) in zip(copies, places):
        copy.wait()
        start = starts[bond, down]
        starts[bond, down] = jnp.where(
            live_of(sizes, bond, down, block), start, jnp.zeros_like(start)
        )


def is_late(code):
    even = lax.rem(lax.axis_index("blk"), 2) == 0
    return code == jnp.where(even, 1, 2)


def list_units(shift, downs, lists):
    channels = shift.shape[0]
    end = channels * downs
    early, late = jnp.int32(0), jnp.int32(0)
    for channel in range(channels):
        code = shift[channel]
        far = is_late(code)
        near = jnp.logical_not(far) & ((code == 1) | (code == 2))
        move = (code == 4).astype(jnp.int32) - (code == 3).astype(jnp.int32)
        opens = jnp.int32(1)
        for down in range(downs):
            source = down + move
            here = jnp.logical_not(far) & (source >= 0) & (source < downs)
            lists[EARLY + CHANNEL, early] = jnp.int32(channel)
            lists[EARLY + KIND, early] = near.astype(jnp.int32)
            lists[EARLY + DOWN, early] = jnp.int32(down)
            lists[EARLY + SOURCE, early] = jnp.where(near, downs + down, source)
            lists[EARLY + OPENS, early] = opens
            lists[LATE + CHANNEL, late] = jnp.int32(channel)
            lists[LATE + KIND, late] = jnp.int32(0)
            lists[LATE + DOWN, late] = jnp.int32(down)
            lists[LATE + SOURCE, late] = jnp.int32(down)
            opens = jnp.where(here, 0, opens)
            early = early + here.astype(jnp.int32)
            late = late + far.astype(jnp.int32)
    lists[EARLY, end] = early
    lists[LATE, end] = late


class Unparted:
    def __init__(self, sums):
        self.sums = sums

    def __getitem__(self, place):
        return self.sums[place[1:]]

    def __setitem__(self, place, value):
        self.sums[place[1:]] = value


def add_units(lists, base, lefts, rights, sources, sums, arrived=None):
    def images(indices):
        units = [
            [lists[base + part, index] for part in (CHANNEL, KIND, DOWN, SOURCE)]
            for index in indices
        ]
        if arrived is not None:
            for index, unit in zip(indices, units):
                pl.when(lists[base + OPENS, index] == 1)(functools.partial(arrived, unit[0]))
        halves = [
            [
                dot(lefts[bond][channel, down], sources[bond, source]).astype(BF16)
                for bond in range(BONDS)
            ]
            for channel, _, down, source in units
        ]
        for (channel, kind, down, _), half in zip(units, halves):
            for bond in range(BONDS):
                sums[kind, bond, down] += dot_by_rows(half[bond], rights[bond][channel, down])

    count = lists[base, lists.shape[1] - 1]
    done = jnp.int32(0)
    for size in (4, 2, 1):
        steps = lax.div(count - done, size)

        def step(index, carry, size=size, done=done):
            first = done + size * index
            images([first + i for i in range(size)])
            return carry

        lax.fori_loop(0, steps, step, 0)
        done = done + size * steps


def fill_sources(own, swapped, sources):
    downs = own.shape[1]
    for bond in range(BONDS):
        for down in range(downs):
            sources[bond, down] = own[bond, down]
            sources[bond, downs + down] = swapped[bond, down]


def opening(shift_held, starts, swapped, *refs):
    held, loaded, (images, near_rest, row, lists, sources, shift, shift_sem, sems) = (
        refs[:4],
        refs[4:8],
        refs[8:],
    )
    shift_copy = pltpu.make_async_copy(shift_held, shift, shift_sem)
    shift_copy.start()
    left_a, right_a, left_b, right_b = loaded
    channels, downs = left_a.shape[0], left_a.shape[1]

    def copies(channel):
        return [
            pltpu.make_async_copy(source.at[channel], target.at[channel], sems.at[channel])
            for source, target in zip(held, loaded)
        ]

    def await_one(channel):
        for copy in copies(channel):
            copy.wait()

    for channel in range(channels):
        for copy in copies(channel):
            copy.start()
    shift_copy.wait()
    list_units(shift, downs, lists)
    images[...] = jnp.zeros_like(images)
    fill_sources(starts, swapped, sources)
    found = []
    for bond in range(BONDS):
        size = jnp.zeros((1, 1), F32)
        for down in range(downs):
            start = starts[bond, down].astype(F32)
            size += total(start * start)
        found.append((bond * BOND_LANES + SIZE, size))
    add_units(lists, EARLY, (left_a, left_b), (right_a, right_b), sources, images, await_one)
    pairs = [(bond, kind) for bond in range(BONDS) for kind in range(2)]
    crosses = totals(
        [
            sum(
                folded(starts[bond, down].astype(F32) * images[kind, bond, down])
                for down in range(downs)
            )
            for bond, kind in pairs
        ]
    )
    for (bond, kind), cross in zip(pairs, crosses):
        found.append((bond * BOND_LANES + START_OWN + kind, cross))
    for bond in range(BONDS):
        size = found[bond][1]
        cross = crosses[2 * bond] + crosses[2 * bond + 1]
        quotient = jnp.where(size > 0.0, cross / jnp.where(size > 0.0, size, 1.0), 0.0)
        found.append((bond * BOND_LANES + QUOTIENT, quotient))
        for down in range(downs):
            image = images[0, bond, down] + images[1, bond, down]
            near_rest[bond, down] = image - quotient * starts[bond, down].astype(F32)
    row[...] = jnp.broadcast_to(in_lanes(row.shape[1], found), row.shape)
    for channel in range(channels):
        pl.when(is_late(shift[channel]))(functools.partial(await_one, channel))


def mixing(mix, env, after, mixed):
    del after
    channels, downs, block = env.shape[0], env.shape[1], env.shape[-1]
    wide = channels * GROUP
    squared = exact_dot(mix[...], mix[...])
    spread_rows = (
        lax.broadcasted_iota(jnp.int32, (wide, channels), 0) // GROUP
        == lax.broadcasted_iota(jnp.int32, (wide, channels), 1)
    ).astype(F32)
    spread_cols = (
        lax.broadcasted_iota(jnp.int32, (channels, wide), 1) // GROUP
        == lax.broadcasted_iota(jnp.int32, (channels, wide), 0)
    ).astype(F32)
    spread = exact_dot(exact_dot(spread_rows, squared), spread_cols)
    same = lax.rem(lax.broadcasted_iota(jnp.int32, (wide, wide), 0), GROUP) == lax.rem(
        lax.broadcasted_iota(jnp.int32, (wide, wide), 1), GROUP
    )
    spread = jnp.where(same, spread, 0.0)
    mix_high = spread.astype(BF16)
    mix_low = (spread - mix_high.astype(F32)).astype(BF16)
    for down in range(downs):
        for group in range(block // GROUP):
            rows = slice(group * GROUP, (group + 1) * GROUP)
            part = env[:, down, rows, :].reshape(wide, block)
            made = dot(mix_high, part) + dot(mix_low, part)
            mixed[:, down, rows, :] = made.astype(BF16).reshape(channels, GROUP, block)


def first_images(
    lists_held,
    sizes_held,
    left_a,
    right_a,
    left_b,
    right_b,
    shifted,
    near_rest,
    rest,
    sent,
    lists,
    sizes,
    sems,
):
    lists_copy = pltpu.make_async_copy(lists_held, lists, sems.at[0])
    lists_copy.start()
    sizes_copy = pltpu.make_async_copy(sizes_held, sizes, sems.at[1])
    sizes_copy.start()
    downs, block = left_a.shape[1], left_a.shape[-1]
    rest[...] = near_rest[...]
    lists_copy.wait()
    add_units(lists, LATE, (left_a, left_b), (right_a, right_b), shifted, Unparted(rest))
    sizes_copy.wait()
    for bond in range(BONDS):
        for down in range(downs):
            left_over = jnp.where(live_of(sizes, bond, down, block), rest[bond, down], 0.0)
            rest[bond, down] = left_over
            sent[bond, down] = left_over.astype(BF16)


def early_seconds(
    lists_held,
    left_a,
    right_a,
    left_b,
    right_b,
    sent,
    swapped,
    starts,
    rest,
    images,
    row_in,
    row,
    sums,
    along,
    sources,
    lists,
    lists_sem,
    sems,
):
    lists_copy = pltpu.make_async_copy(lists_held, lists, lists_sem)
    lists_copy.start()
    downs = left_a.shape[1]
    copies = [
        pltpu.make_async_copy(source.at[BONDS - 1], along.at[index], sems.at[index])
        for index, source in enumerate((starts, sent))
    ]
    for copy in copies:
        copy.start()
    sums[...] = jnp.zeros_like(sums)
    fill_sources(sent, swapped, sources)
    lists_copy.wait()
    add_units(lists, EARLY, (left_a, left_b), (right_a, right_b), sources, Unparted(sums))
    places, parts = [], []
    for bond in range(BONDS):
        folds = {place: 0.0 for place in (REST, START_REST, REST_OWN, REST_SWAPPED)}
        for down in range(downs):
            left_over = rest[bond, down]
            folds[START_REST] += folded(left_over * starts[bond, down].astype(F32))
            folds[REST] += folded(left_over * left_over)
            for kind in range(2):
                folds[REST_OWN + kind] += folded(left_over * images[kind, bond, down])
        places += [bond * BOND_LANES + place for place in folds]
        parts += folds.values()
    found = list(zip(places, totals(parts)))
    row[...] = row_in[...] + jnp.broadcast_to(in_lanes(row.shape[1], found), row.shape)
    for copy in copies:
        copy.wait()


def late_seconds(
    lists_held,
    left_a,
    right_a,
    left_b,
    right_b,
    shifted,
    starts,
    rest,
    early_sums,
    row_in,
    row,
    sums,
    lists,
    lists_sem,
):
    lists_copy = pltpu.make_async_copy(lists_held, lists, lists_sem)
    lists_copy.start()
    downs = left_a.shape[1]
    sums[...] = early_sums[...]
    lists_copy.wait()
    add_units(lists, LATE, (left_a, left_b), (right_a, right_b), shifted, Unparted(sums))
    places, parts = [], []
    for bond in range(BONDS):
        of_rest, of_start = 0.0, 0.0
        for down in range(downs):
            image = sums[bond, down]
            of_rest += folded(rest[bond, down] * image)
            of_start += folded(starts[bond, down].astype(F32) * image)
        places += [bond * BOND_LANES + REST_IMAGE, bond * BOND_LANES + START_IMAGE]
        parts += [of_rest, of_start]
    found = list(zip(places, totals(parts)))
    row[...] = jnp.broadcast_to(row_in[0:1, :] + in_lanes(row.shape[1], found), row.shape)


def ritz(numbers, bond, first, ups, place):
    lane = lax.broadcasted_iota(jnp.int32, (1, numbers.shape[1]), 1)
    inside = (lane >= first) & (lane < first + ups)

    def part(index):
        at = bond * BOND_LANES + index
        return numbers[at : at + 1]

    def over_ups(values):
        return jnp.sum(jnp.where(inside, values, 0.0), axis=1, keepdims=True)

    size = part(SIZE)
    quotient = part(QUOTIENT)
    rest_sq = part(REST)
    start_rest = part(START_REST)
    low = pltpu.roll(quotient, 1, 1)
    high = pltpu.roll(quotient, quotient.shape[1] - 1, 1)
    even = (lane & 1) == 0
    none_low, none_high = lane == first, lane == first + ups - 1
    norm_sq = over_ups(size)
    alpha_zero = over_ups(size * quotient + start_rest) / norm_sq
    off = quotient - alpha_zero
    off_low = jnp.where(none_low, 0.0, low - alpha_zero)
    off_high = jnp.where(none_high, 0.0, high - alpha_zero)
    off_swapped = jnp.where(even, off_high, off_low)
    off_shifted = jnp.where(even, off_low, off_high)
    along_start = jnp.where(size > 0.0, start_rest / jnp.where(size > 0.0, size, 1.0), 0.0)
    across_sq = jnp.maximum(rest_sq - start_rest * along_start, 0.0)
    residual_sq = over_ups(across_sq + size * (off + along_start) * (off + along_start))
    crossed = part(REST_IMAGE) + off * part(START_IMAGE)
    rest_of = [part(REST_OWN), part(REST_SWAPPED)]
    start_of = [part(START_OWN), part(START_SWAPPED)]
    rest_of.append(rest_sq + quotient * start_rest - rest_of[0] - rest_of[1])
    start_of.append(start_rest + quotient * size - start_of[0] - start_of[1])
    for factor, of_rest, of_start in zip((off, off_swapped, off_shifted), rest_of, start_of):
        crossed += factor * (of_rest + off * of_start)
    alpha_one = over_ups(crossed) / residual_sq
    beta_sq = residual_sq / norm_sq
    beta = jnp.sqrt(beta_sq)
    spread = 0.5 * (alpha_zero - alpha_one)
    energy = 0.5 * (alpha_zero + alpha_one) - jnp.sqrt(spread * spread + beta_sq)
    weight_one = energy - alpha_zero
    length = jnp.sqrt(beta_sq + weight_one * weight_one)
    of_rest = weight_one / (beta * length)
    own_off = jnp.sum(jnp.where(lane == first + place, off, 0.0), axis=1, keepdims=True)
    return energy, beta / length + of_rest * own_off, of_rest


def finish(
    factor,
    ups,
    numbers,
    starts_held,
    rest_held,
    along_held,
    edge_held,
    mixed_held,
    ground_a,
    ground_b,
    energies_out,
    boundary,
    energies,
    starts,
    rest,
    along,
    edge,
    mixed,
    made,
    grounds,
    in_sems,
    mixed_sems,
    out_sems,
):
    channels, downs = mixed.shape[0], mixed.shape[1]

    def arrival(index, source, target):
        copy = pltpu.make_async_copy(source, target, in_sems.at[index])
        copy.start()
        return copy

    first = [
        [
            arrival(0 + 4 * down, starts_held.at[0, down], starts.at[0, down]),
            arrival(1 + 4 * down, rest_held.at[0, down], rest.at[0, down]),
            arrival(2 + 4 * down, along_held.at[:, down], along.at[:, down]),
            arrival(3 + 4 * down, edge_held.at[down], edge.at[down]),
        ]
        for down in range(downs)
    ]
    arrivals = [
        pltpu.make_async_copy(mixed_held.at[index], mixed.at[index], mixed_sems.at[index])
        for index in range(channels)
    ]
    for copy in arrivals[:BATCH]:
        copy.start()
    second = [
        arrival(4 * downs, starts_held.at[1], starts.at[1]),
        arrival(4 * downs + 1, rest_held.at[1], rest.at[1]),
    ]
    for copy in arrivals[BATCH:]:
        copy.start()
    devices, width = numbers.shape
    segments = devices // ups
    seg, blk = lax.axis_index("seg"), lax.axis_index("blk")
    after = jnp.minimum(seg + 1, segments - 1)
    padding = [jnp.zeros((-devices % width, width), F32)] if devices % width else []
    by_place = jnp.concatenate([numbers[...], *padding]).T
    solves = [
        ritz(by_place, bond, at * ups, ups, blk) for bond, at in ((0, seg), (1, seg), (1, after))
    ]
    energy, of_start, of_rest = zip(*solves)
    lane = lax.broadcasted_iota(jnp.int32, energies.shape, 1)
    energies[...] = jnp.where(lane == 0, energy[0], energy[1])
    last = seg == segments - 1
    out_copies = [pltpu.make_async_copy(energies, energies_out, in_sems.at[4 * downs + 2])]
    out_copies[0].start()

    def leave(index, source, target):
        copy = pltpu.make_async_copy(source, target, out_sems.at[index])
        copy.start()
        out_copies.append(copy)

    def ground_of(bond, target):
        for down in range(downs):
            start = starts[bond, down].astype(F32)
            grounds[bond, down] = of_start[bond] * start + of_rest[bond] * rest[bond, down]
        leave(channels + bond, grounds.at[bond], target)

    products = []
    for down in range(downs):
        for copy in first[down]:
            copy.wait()
        start = starts[0, down].astype(F32)
        ground = of_start[0] * start + of_rest[0] * rest[0, down]
        grounds[0, down] = ground
        found = of_start[2] * along[0, down].astype(F32) + of_rest[2] * along[1, down].astype(F32)
        state = jnp.where(last, edge[down], found.astype(BF16))
        product = (dot(ground.astype(BF16), state) * factor).astype(BF16)
        products.append((product, product.T))
    leave(channels, grounds.at[0], ground_a)
    halves = {}

    def last_product(group):
        for channel in group:
            for down, (_, turned) in enumerate(products):
                made[channel, down] = dot(turned, halves[channel, down]).astype(BF16)
        for channel in group:
            leave(channel, made.at[channel], boundary.at[channel])

    groups = []
    while sum(map(len, groups)) < channels:
        at = sum(map(len, groups))
        groups.append(range(at, at + min(BATCH, (channels - at + 1) // 2)))
    for index, group in enumerate(groups):
        for channel in group:
            arrivals[channel].wait()
        for down, (product, _) in enumerate(products):
            block = product.shape[0]
            stacked = mixed[group.start : group.stop, down].reshape(len(group) * block, block)
            half = dot(stacked, product).astype(BF16)
            for place, channel in enumerate(group):
                halves[channel, down] = half[place * block : (place + 1) * block]
        if index > 0:
            last_product(groups[index - 1])
        if index == min(1, len(groups) - 1):
            for copy in second:
                copy.wait()
            ground_of(1, ground_b)
    last_product(groups[-1])
    for copy in out_copies:
        copy.wait()


def swapped_pairs(block):
    devices = range(lax.axis_size("blk"))
    return lax.ppermute(block, "blk", [(i, i ^ 1) for i in devices if i ^ 1 in devices])


def shifted_pairs(block):
    devices = range(lax.axis_size("blk"))
    pairs = [(i, i + 1) for i in devices if i % 2 == 1 and i + 1 in devices]
    return lax.ppermute(block, "blk", pairs + [(j, i) for i, j in pairs])


def from_right_segment(block):
    segments = lax.axis_size("seg")
    return lax.ppermute(block, "seg", [(i + 1, i) for i in range(segments - 1)])


def local(
    guess_a,
    guess_b,
    left_env_a,
    right_env_a,
    left_env_b,
    right_env_b,
    channel_mix,
    term_shift,
    sector_sizes,
    edge_state,
):
    block = guess_a.shape[-1]
    downs = guess_a.shape[2]
    channels = left_env_a.shape[1]
    ups = lax.axis_size("blk")
    devices = ups * lax.axis_size("seg")
    pair = (downs, block, block)
    both = (BONDS,) + pair
    env_shape = (channels, downs, block, block)
    held = [in_hbm(env.reshape(env_shape)) for env in (left_env_a, right_env_a, left_env_b, right_env_b)]
    bits = 2 * downs * block * block
    env_bytes = channels * bits
    apply_flops = 4 * channels * downs * block**3
    sizes = in_hbm(sector_sizes.transpose(0, 2, 3, 1))
    tile = jax.ShapeDtypeStruct((8, 128), F32)

    (starts,) = call(
        masked_starts,
        "masked_starts",
        [HBM, HBM, HBM],
        [(VMEM, pltpu.VMEM(both, BF16))],
        [pltpu.SMEM(sizes.shape, jnp.int32), pltpu.SemaphoreType.DMA(()), pltpu.SemaphoreType.DMA((BONDS, downs))],
        4 * downs * block * block,
        4 * bits,
    )(sizes, in_hbm(guess_a.reshape(pair)), in_hbm(guess_b.reshape(pair)))
    swapped, shifted = swapped_pairs(starts), shifted_pairs(starts)

    list_shape = (LIST_ROWS, channels * downs + 1)
    sources = pltpu.VMEM((BONDS, 2 * downs, block, block), BF16)
    *loaded, images, near_rest, row, lists = call(
        opening,
        "opening",
        [HBM, VMEM, VMEM] + [HBM] * 4,
        [(VMEM, pltpu.VMEM(env_shape, BF16))] * 4
        + [
            (VMEM, pltpu.VMEM((2,) + both, F32)),
            (VMEM, pltpu.VMEM(both, F32)),
            (VMEM, tile),
            (SMEM, jax.ShapeDtypeStruct(list_shape, jnp.int32)),
        ],
        [
            sources,
            pltpu.SMEM((channels,), jnp.int32),
            pltpu.SemaphoreType.DMA(()),
            pltpu.SemaphoreType.DMA((channels,)),
        ],
        apply_flops,
        5 * env_bytes,
    )(in_hbm(term_shift), starts, swapped, *held)

    rest, sent = call(
        first_images,
        "first_images",
        [VMEM, HBM] + [VMEM] * 6,
        [
            (VMEM, pltpu.VMEM(both, F32)),
            (VMEM, pltpu.VMEM(both, BF16)),
        ],
        [
            pltpu.SMEM(list_shape, jnp.int32),
            pltpu.SMEM(sizes.shape, jnp.int32),
            pltpu.SemaphoreType.DMA((2,)),
        ],
        apply_flops,
        env_bytes,
    )(lists, sizes, *loaded, shifted, near_rest)
    swapped, shifted = swapped_pairs(sent), shifted_pairs(sent)
    row, sums, along = call(
        early_seconds,
        "early_seconds",
        [VMEM] * 11,
        [
            (VMEM, tile),
            (VMEM, pltpu.VMEM(both, F32)),
            (HBM, jax.ShapeDtypeStruct((2,) + pair, BF16)),
        ],
        [
            sources,
            pltpu.SMEM(list_shape, jnp.int32),
            pltpu.SemaphoreType.DMA(()),
            pltpu.SemaphoreType.DMA((2,)),
        ],
        apply_flops,
        env_bytes,
    )(lists, *loaded, sent, swapped, starts, rest, images, row)
    from_next = from_right_segment(along)
    (row,) = call(
        late_seconds,
        "late_seconds",
        [VMEM] * 10,
        [(VMEM, pltpu.VMEM((devices, 128), F32))],
        [
            pltpu.VMEM(both, F32),
            pltpu.SMEM(list_shape, jnp.int32),
            pltpu.SemaphoreType.DMA(()),
        ],
        apply_flops,
        env_bytes,
    )(lists, *loaded, shifted, starts, rest, sums, row)
    numbers = lax.all_to_all(row, ("seg", "blk"), 0, 0, tiled=True)
    (mixed,) = call(
        mixing,
        "mixing",
        [VMEM, VMEM, HBM],
        [(VMEM, jax.ShapeDtypeStruct(env_shape, BF16))],
        [],
        4 * channels * channels * GROUP * downs * block * block,
        2 * env_bytes,
    )(channel_mix, loaded[0], row)
    state32 = jax.ShapeDtypeStruct(pair, F32)
    ground_a, ground_b, energies, boundary = call(
        functools.partial(finish, 1.0 / block, ups),
        "finish",
        [VMEM] + [HBM] * 5,
        [
            (HBM, state32),
            (HBM, state32),
            (HBM, jax.ShapeDtypeStruct((1, 2), F32)),
            (HBM, jax.ShapeDtypeStruct(env_shape, BF16)),
        ],
        [
            pltpu.VMEM((1, 2), F32),
            pltpu.VMEM(both, BF16),
            pltpu.VMEM(both, F32),
            pltpu.VMEM((2,) + pair, BF16),
            pltpu.VMEM(pair, BF16),
            pltpu.VMEM(env_shape, BF16),
            pltpu.VMEM(env_shape, BF16),
            pltpu.VMEM(both, F32),
            pltpu.SemaphoreType.DMA((4 * downs + 3,)),
            pltpu.SemaphoreType.DMA((channels,)),
            pltpu.SemaphoreType.DMA((channels + BONDS,)),
        ],
        apply_flops,
        2 * env_bytes,
    )(
        numbers,
        *(in_hbm(x) for x in (starts, rest, from_next, edge_state.reshape(pair), mixed)),
    )
    return (
        ground_a.reshape(guess_a.shape),
        ground_b.reshape(guess_b.shape),
        energies,
        boundary.reshape(left_env_a.shape),
    )


def solution(mesh):
    placed = (
        P("seg", "blk", None, None, None),
        P("seg", "blk", None, None, None),
        P("seg", None, "blk", None, None, None),
        P("seg", None, "blk", None, None, None),
        P("seg", None, "blk", None, None, None),
        P("seg", None, "blk", None, None, None),
        P(),
        P(),
        P("seg", None, "blk", None),
        P("blk", None, None, None),
    )
    return jax.shard_map(
        local,
        mesh=mesh,
        in_specs=placed,
        out_specs=(
            P("seg", "blk", None, None, None),
            P("seg", "blk", None, None, None),
            P("seg", None),
            P("seg", None, "blk", None, None, None),
        ),
        check_vma=False,
    )
```

```python
import functools

import jax
import jax.numpy as jnp
from jax import lax
from jax.experimental import pallas as pl
from jax.experimental.pallas import tpu as pltpu
from jax.sharding import PartitionSpec as P

F32 = jnp.float32
BF16 = jnp.bfloat16
VMEM = pl.BlockSpec(memory_space=pltpu.VMEM)
SMEM = pl.BlockSpec(memory_space=pltpu.SMEM)
HBM = pl.BlockSpec(memory_space=pltpu.HBM)
MIB = 1 << 20
GROUP = 16
BATCH = 6
BONDS = 2

CHANNEL, KIND, DOWN, SOURCE, OPENS = range(5)
EARLY, LATE = 0, OPENS + 1
LIST_ROWS = LATE + SOURCE + 1


(
    SIZE,
    QUOTIENT,
    REST,
    START_REST,
    REST_IMAGE,
    START_IMAGE,
    REST_OWN,
    REST_SWAPPED,
    START_OWN,
    START_SWAPPED,
) = range(10)
BOND_LANES = 64


def call(body, name, ins, outs, scratch, flops, moved, limit=20 * MIB):
    return pl.pallas_call(
        body,
        name=name,
        in_specs=ins,
        out_specs=tuple(spec for spec, _ in outs),
        out_shape=tuple(shape for _, shape in outs),
        scratch_shapes=scratch,
        cost_estimate=pl.CostEstimate(flops=flops, bytes_accessed=moved, transcendentals=0),
        compiler_params=pltpu.CompilerParams(vmem_limit_bytes=limit),
    )


def in_hbm(array):
    return pltpu.with_memory_space_constraint(array, pltpu.HBM)


def live(rows, cols, block):
    row = lax.broadcasted_iota(jnp.int32, (block, block), 0)
    col = lax.broadcasted_iota(jnp.int32, (block, block), 1)
    return (row < rows) & (col < cols)


def live_of(sizes, bond, down, block):
    return live(sizes[0, 0, down, 2 * bond], sizes[0, 0, down, 2 * bond + 1], block)


def dot(left, right):
    return jnp.dot(left, right, preferred_element_type=F32)


def dot_by_rows(left, right):
    return lax.dot_general(left, right, (((1,), (1,)), ((), ())), preferred_element_type=F32)


def exact_dot(left, right):
    return jnp.dot(left, right, precision=lax.Precision.HIGHEST, preferred_element_type=F32)


def total(array):
    return jnp.sum(jnp.sum(array, axis=0, keepdims=True), axis=1, keepdims=True)


def folded(array):
    return jnp.sum(array.reshape(-1, 8, array.shape[-1]), axis=0)


def totals(parts):
    rows = parts[0].shape[0]
    by_row = jnp.sum(jnp.concatenate(parts), axis=1, keepdims=True)
    return [
        jnp.sum(by_row[i * rows : (i + 1) * rows], axis=0, keepdims=True) for i in range(len(parts))
    ]


def in_lanes(width, pairs):
    lane = lax.broadcasted_iota(jnp.int32, (1, width), 1)
    row = jnp.zeros((1, width), F32)
    for place, value in pairs:
        row = jnp.where(lane == place, value, row)
    return row


def masked_starts(sizes_held, guess_a, guess_b, starts, sizes, size_sem, sems):
    sizes_copy = pltpu.make_async_copy(sizes_held, sizes, size_sem)
    sizes_copy.start()
    downs, block = starts.shape[1], starts.shape[-1]
    copies = [
        pltpu.make_async_copy(guess, starts.at[bond], sems.at[bond])
        for bond, guess in enumerate((guess_a, guess_b))
    ]
    for copy in copies:
        copy.start()
    sizes_copy.wait()
    for bond, down in [(bond, down) for bond in range(BONDS) for down in range(downs)]:
        if down == 0:
            copies[bond].wait()
        start = starts[bond, down]
        starts[bond, down] = jnp.where(
            live_of(sizes, bond, down, block), start, jnp.zeros_like(start)
        )


def is_late(code):
    even = lax.rem(lax.axis_index("blk"), 2) == 0
    return code == jnp.where(even, 1, 2)


def list_units(shift, downs, lists):
    channels = shift.shape[0]
    end = channels * downs
    early, late = jnp.int32(0), jnp.int32(0)
    for channel in range(channels):
        code = shift[channel]
        far = is_late(code)
        near = jnp.logical_not(far) & ((code == 1) | (code == 2))
        move = (code == 4).astype(jnp.int32) - (code == 3).astype(jnp.int32)
        opens = jnp.int32(1)
        for down in range(downs):
            source = down + move
            here = jnp.logical_not(far) & (source >= 0) & (source < downs)
            lists[EARLY + CHANNEL, early] = jnp.int32(channel)
            lists[EARLY + KIND, early] = near.astype(jnp.int32)
            lists[EARLY + DOWN, early] = jnp.int32(down)
            lists[EARLY + SOURCE, early] = jnp.where(near, downs + down, source)
            lists[EARLY + OPENS, early] = opens
            lists[LATE + CHANNEL, late] = jnp.int32(channel)
            lists[LATE + KIND, late] = jnp.int32(0)
            lists[LATE + DOWN, late] = jnp.int32(down)
            lists[LATE + SOURCE, late] = jnp.int32(down)
            opens = jnp.where(here, 0, opens)
            early = early + here.astype(jnp.int32)
            late = late + far.astype(jnp.int32)
    lists[EARLY, end] = early
    lists[LATE, end] = late


class Unparted:
    def __init__(self, sums):
        self.sums = sums

    def __getitem__(self, place):
        return self.sums[place[1:]]

    def __setitem__(self, place, value):
        self.sums[place[1:]] = value


def add_units(lists, base, lefts, rights, sources, sums, arrived=None):
    def images(indices):
        units = [
            [lists[base + part, index] for part in (CHANNEL, KIND, DOWN, SOURCE)]
            for index in indices
        ]
        if arrived is not None:
            for index, unit in zip(indices, units):
                pl.when(lists[base + OPENS, index] == 1)(functools.partial(arrived, unit[0]))
        halves = [
            [
                dot(lefts[bond][channel, down], sources[bond, source]).astype(BF16)
                for bond in range(BONDS)
            ]
            for channel, _, down, source in units
        ]
        for (channel, kind, down, _), half in zip(units, halves):
            for bond in range(BONDS):
                sums[kind, bond, down] += dot_by_rows(half[bond], rights[bond][channel, down])

    count = lists[base, lists.shape[1] - 1]
    done = jnp.int32(0)
    for size in (4, 2, 1):
        steps = lax.div(count - done, size)

        def step(index, carry, size=size, done=done):
            first = done + size * index
            images([first + i for i in range(size)])
            return carry

        lax.fori_loop(0, steps, step, 0)
        done = done + size * steps


def fill_sources(own, swapped, sources):
    downs = own.shape[1]
    for bond in range(BONDS):
        for down in range(downs):
            sources[bond, down] = own[bond, down]
            sources[bond, downs + down] = swapped[bond, down]


def opening(shift_held, starts, swapped, *refs):
    held, loaded, (images, near_rest, row, lists, sources, shift, shift_sem, sems) = (
        refs[:4],
        refs[4:8],
        refs[8:],
    )
    shift_copy = pltpu.make_async_copy(shift_held, shift, shift_sem)
    shift_copy.start()
    left_a, right_a, left_b, right_b = loaded
    channels, downs = left_a.shape[0], left_a.shape[1]

    def copies(channel):
        return [
            pltpu.make_async_copy(source.at[channel], target.at[channel], sems.at[channel])
            for source, target in zip(held, loaded)
        ]

    def await_one(channel):
        for copy in copies(channel):
            copy.wait()

    for channel in range(channels):
        for copy in copies(channel):
            copy.start()
    shift_copy.wait()
    list_units(shift, downs, lists)
    images[...] = jnp.zeros_like(images)
    fill_sources(starts, swapped, sources)
    found = []
    for bond in range(BONDS):
        size = jnp.zeros((1, 1), F32)
        for down in range(downs):
            start = starts[bond, down].astype(F32)
            size += total(start * start)
        found.append((bond * BOND_LANES + SIZE, size))
    add_units(lists, EARLY, (left_a, left_b), (right_a, right_b), sources, images, await_one)
    pairs = [(bond, kind) for bond in range(BONDS) for kind in range(2)]
    crosses = totals(
        [
            sum(
                folded(starts[bond, down].astype(F32) * images[kind, bond, down])
                for down in range(downs)
            )
            for bond, kind in pairs
        ]
    )
    for (bond, kind), cross in zip(pairs, crosses):
        found.append((bond * BOND_LANES + START_OWN + kind, cross))
    for bond in range(BONDS):
        size = found[bond][1]
        cross = crosses[2 * bond] + crosses[2 * bond + 1]
        quotient = jnp.where(size > 0.0, cross / jnp.where(size > 0.0, size, 1.0), 0.0)
        found.append((bond * BOND_LANES + QUOTIENT, quotient))
        for down in range(downs):
            image = images[0, bond, down] + images[1, bond, down]
            near_rest[bond, down] = image - quotient * starts[bond, down].astype(F32)
    row[...] = jnp.broadcast_to(in_lanes(row.shape[1], found), row.shape)
    for channel in range(channels):
        pl.when(is_late(shift[channel]))(functools.partial(await_one, channel))


def mixing(mix, env, after, mixed):
    del after
    channels, downs, block = env.shape[0], env.shape[1], env.shape[-1]
    wide = channels * GROUP
    squared = exact_dot(mix[...], mix[...])
    spread_rows = (
        lax.broadcasted_iota(jnp.int32, (wide, channels), 0) // GROUP
        == lax.broadcasted_iota(jnp.int32, (wide, channels), 1)
    ).astype(F32)
    spread_cols = (
        lax.broadcasted_iota(jnp.int32, (channels, wide), 1) // GROUP
        == lax.broadcasted_iota(jnp.int32, (channels, wide), 0)
    ).astype(F32)
    spread = exact_dot(exact_dot(spread_rows, squared), spread_cols)
    same = lax.rem(lax.broadcasted_iota(jnp.int32, (wide, wide), 0), GROUP) == lax.rem(
        lax.broadcasted_iota(jnp.int32, (wide, wide), 1), GROUP
    )
    spread = jnp.where(same, spread, 0.0)
    mix_high = spread.astype(BF16)
    mix_low = (spread - mix_high.astype(F32)).astype(BF16)
    for down in range(downs):
        for group in range(block // GROUP):
            rows = slice(group * GROUP, (group + 1) * GROUP)
            part = env[:, down, rows, :].reshape(wide, block)
            made = dot(mix_high, part) + dot(mix_low, part)
            mixed[:, down, rows, :] = made.astype(BF16).reshape(channels, GROUP, block)


def first_images(
    lists_held,
    sizes_held,
    left_a,
    right_a,
    left_b,
    right_b,
    shifted,
    near_rest,
    rest,
    sent,
    lists,
    sizes,
    sems,
):
    lists_copy = pltpu.make_async_copy(lists_held, lists, sems.at[0])
    lists_copy.start()
    sizes_copy = pltpu.make_async_copy(sizes_held, sizes, sems.at[1])
    sizes_copy.start()
    downs, block = left_a.shape[1], left_a.shape[-1]
    rest[...] = near_rest[...]
    lists_copy.wait()
    add_units(lists, LATE, (left_a, left_b), (right_a, right_b), shifted, Unparted(rest))
    sizes_copy.wait()
    for bond in range(BONDS):
        for down in range(downs):
            left_over = jnp.where(live_of(sizes, bond, down, block), rest[bond, down], 0.0)
            rest[bond, down] = left_over
            sent[bond, down] = left_over.astype(BF16)


def early_seconds(
    lists_held,
    left_a,
    right_a,
    left_b,
    right_b,
    sent,
    swapped,
    starts,
    rest,
    images,
    row_in,
    row,
    sums,
    along,
    sources,
    lists,
    lists_sem,
    sems,
):
    lists_copy = pltpu.make_async_copy(lists_held, lists, lists_sem)
    lists_copy.start()
    downs = left_a.shape[1]
    copies = [
        pltpu.make_async_copy(source.at[BONDS - 1], along.at[index], sems.at[index])
        for index, source in enumerate((starts, sent))
    ]
    for copy in copies:
        copy.start()
    sums[...] = jnp.zeros_like(sums)
    fill_sources(sent, swapped, sources)
    lists_copy.wait()
    add_units(lists, EARLY, (left_a, left_b), (right_a, right_b), sources, Unparted(sums))
    places, parts = [], []
    for bond in range(BONDS):
        folds = {place: 0.0 for place in (REST, START_REST, REST_OWN, REST_SWAPPED)}
        for down in range(downs):
            left_over = rest[bond, down]
            folds[START_REST] += folded(left_over * starts[bond, down].astype(F32))
            folds[REST] += folded(left_over * left_over)
            for kind in range(2):
                folds[REST_OWN + kind] += folded(left_over * images[kind, bond, down])
        places += [bond * BOND_LANES + place for place in folds]
        parts += folds.values()
    found = list(zip(places, totals(parts)))
    row[...] = row_in[...] + jnp.broadcast_to(in_lanes(row.shape[1], found), row.shape)
    for copy in copies:
        copy.wait()


def late_seconds(
    lists_held,
    left_a,
    right_a,
    left_b,
    right_b,
    shifted,
    starts,
    rest,
    early_sums,
    row_in,
    row,
    sums,
    lists,
    lists_sem,
):
    lists_copy = pltpu.make_async_copy(lists_held, lists, lists_sem)
    lists_copy.start()
    downs = left_a.shape[1]
    sums[...] = early_sums[...]
    lists_copy.wait()
    add_units(lists, LATE, (left_a, left_b), (right_a, right_b), shifted, Unparted(sums))
    places, parts = [], []
    for bond in range(BONDS):
        of_rest, of_start = 0.0, 0.0
        for down in range(downs):
            image = sums[bond, down]
            of_rest += folded(rest[bond, down] * image)
            of_start += folded(starts[bond, down].astype(F32) * image)
        places += [bond * BOND_LANES + REST_IMAGE, bond * BOND_LANES + START_IMAGE]
        parts += [of_rest, of_start]
    found = list(zip(places, totals(parts)))
    row[...] = jnp.broadcast_to(row_in[0:1, :] + in_lanes(row.shape[1], found), row.shape)


def ritz(numbers, bond, first, ups, place):
    lane = lax.broadcasted_iota(jnp.int32, (1, numbers.shape[1]), 1)
    inside = (lane >= first) & (lane < first + ups)

    def part(index):
        at = bond * BOND_LANES + index
        return numbers[at : at + 1]

    def over_ups(values):
        return jnp.sum(jnp.where(inside, values, 0.0), axis=1, keepdims=True)

    size = part(SIZE)
    quotient = part(QUOTIENT)
    rest_sq = part(REST)
    start_rest = part(START_REST)
    low = pltpu.roll(quotient, 1, 1)
    high = pltpu.roll(quotient, quotient.shape[1] - 1, 1)
    even = (lane & 1) == 0
    none_low, none_high = lane == first, lane == first + ups - 1
    norm_sq = over_ups(size)
    alpha_zero = over_ups(size * quotient + start_rest) / norm_sq
    off = quotient - alpha_zero
    off_low = jnp.where(none_low, 0.0, low - alpha_zero)
    off_high = jnp.where(none_high, 0.0, high - alpha_zero)
    off_swapped = jnp.where(even, off_high, off_low)
    off_shifted = jnp.where(even, off_low, off_high)
    along_start = jnp.where(size > 0.0, start_rest / jnp.where(size > 0.0, size, 1.0), 0.0)
    across_sq = jnp.maximum(rest_sq - start_rest * along_start, 0.0)
    residual_sq = over_ups(across_sq + size * (off + along_start) * (off + along_start))
    crossed = part(REST_IMAGE) + off * part(START_IMAGE)
    rest_of = [part(REST_OWN), part(REST_SWAPPED)]
    start_of = [part(START_OWN), part(START_SWAPPED)]
    rest_of.append(rest_sq + quotient * start_rest - rest_of[0] - rest_of[1])
    start_of.append(start_rest + quotient * size - start_of[0] - start_of[1])
    for factor, of_rest, of_start in zip((off, off_swapped, off_shifted), rest_of, start_of):
        crossed += factor * (of_rest + off * of_start)
    alpha_one = over_ups(crossed) / residual_sq
    beta_sq = residual_sq / norm_sq
    beta = jnp.sqrt(beta_sq)
    spread = 0.5 * (alpha_zero - alpha_one)
    energy = 0.5 * (alpha_zero + alpha_one) - jnp.sqrt(spread * spread + beta_sq)
    weight_one = energy - alpha_zero
    length = jnp.sqrt(beta_sq + weight_one * weight_one)
    of_rest = weight_one / (beta * length)
    own_off = jnp.sum(jnp.where(lane == first + place, off, 0.0), axis=1, keepdims=True)
    return energy, beta / length + of_rest * own_off, of_rest


def finish(
    factor,
    ups,
    numbers,
    starts_held,
    rest_held,
    along_held,
    edge_held,
    mixed_held,
    ground_a,
    ground_b,
    energies_out,
    boundary,
    energies,
    starts,
    rest,
    along,
    edge,
    mixed,
    made,
    grounds,
    in_sems,
    mixed_sems,
    out_sems,
):
    channels, downs = mixed.shape[0], mixed.shape[1]

    def arrival(index, source, target):
        copy = pltpu.make_async_copy(source, target, in_sems.at[index])
        copy.start()
        return copy

    first = [
        arrival(0, starts_held.at[0], starts.at[0]),
        arrival(1, rest_held.at[0], rest.at[0]),
        arrival(2, along_held, along),
        arrival(3, edge_held, edge),
    ]
    groups = []
    while sum(map(len, groups)) < channels:
        at = sum(map(len, groups))
        groups.append(range(at, at + min(BATCH, (channels - at + 1) // 2)))

    def part(array, group):
        return array.at[group.start : group.stop]

    arrivals = [
        pltpu.make_async_copy(part(mixed_held, group), part(mixed, group), mixed_sems.at[index])
        for index, group in enumerate(groups)
    ]
    arrivals[0].start()
    second = [arrival(4, starts_held.at[1], starts.at[1]), arrival(5, rest_held.at[1], rest.at[1])]
    for copy in arrivals[1:]:
        copy.start()
    devices, width = numbers.shape
    segments = devices // ups
    seg, blk = lax.axis_index("seg"), lax.axis_index("blk")
    after = jnp.minimum(seg + 1, segments - 1)
    padding = [jnp.zeros((-devices % width, width), F32)] if devices % width else []
    by_place = jnp.concatenate([numbers[...], *padding]).T
    solves = [
        ritz(by_place, bond, at * ups, ups, blk) for bond, at in ((0, seg), (1, seg), (1, after))
    ]
    energy, of_start, of_rest = zip(*solves)
    lane = lax.broadcasted_iota(jnp.int32, energies.shape, 1)
    energies[...] = jnp.where(lane == 0, energy[0], energy[1])
    last = seg == segments - 1
    out_copies = [pltpu.make_async_copy(energies, energies_out, in_sems.at[6])]
    out_copies[0].start()

    def leave(index, source, target):
        copy = pltpu.make_async_copy(source, target, out_sems.at[index])
        copy.start()
        out_copies.append(copy)

    def ground_of(bond, target):
        for down in range(downs):
            start = starts[bond, down].astype(F32)
            grounds[bond, down] = of_start[bond] * start + of_rest[bond] * rest[bond, down]
        leave(channels + bond, grounds.at[bond], target)

    for copy in first:
        copy.wait()
    products = []
    for down in range(downs):
        start = starts[0, down].astype(F32)
        ground = of_start[0] * start + of_rest[0] * rest[0, down]
        grounds[0, down] = ground
        found = of_start[2] * along[0, down].astype(F32) + of_rest[2] * along[1, down].astype(F32)
        state = jnp.where(last, edge[down], found.astype(BF16))
        product = (dot(ground.astype(BF16), state) * factor).astype(BF16)
        products.append((product, product.T))
    leave(channels, grounds.at[0], ground_a)
    halves = {}

    def last_product(index):
        for channel in groups[index]:
            for down, (_, turned) in enumerate(products):
                made[channel, down] = dot(turned, halves[channel, down]).astype(BF16)
        leave(index, part(made, groups[index]), part(boundary, groups[index]))

    for index, group in enumerate(groups):
        arrivals[index].wait()
        for down, (product, _) in enumerate(products):
            block = product.shape[0]
            stacked = mixed[group.start : group.stop, down].reshape(len(group) * block, block)
            half = dot(stacked, product).astype(BF16)
            for place, channel in enumerate(group):
                halves[channel, down] = half[place * block : (place + 1) * block]
        if index > 0:
            last_product(index - 1)
        if index == min(1, len(groups) - 1):
            for copy in second:
                copy.wait()
            ground_of(1, ground_b)
    last_product(len(groups) - 1)
    for copy in out_copies:
        copy.wait()


def swapped_pairs(block):
    devices = range(lax.axis_size("blk"))
    return lax.ppermute(block, "blk", [(i, i ^ 1) for i in devices if i ^ 1 in devices])


def shifted_pairs(block):
    devices = range(lax.axis_size("blk"))
    pairs = [(i, i + 1) for i in devices if i % 2 == 1 and i + 1 in devices]
    return lax.ppermute(block, "blk", pairs + [(j, i) for i, j in pairs])


def from_right_segment(block):
    segments = lax.axis_size("seg")
    return lax.ppermute(block, "seg", [(i + 1, i) for i in range(segments - 1)])


def local(
    guess_a,
    guess_b,
    left_env_a,
    right_env_a,
    left_env_b,
    right_env_b,
    channel_mix,
    term_shift,
    sector_sizes,
    edge_state,
):
    block = guess_a.shape[-1]
    downs = guess_a.shape[2]
    channels = left_env_a.shape[1]
    ups = lax.axis_size("blk")
    devices = ups * lax.axis_size("seg")
    pair = (downs, block, block)
    both = (BONDS,) + pair
    env_shape = (channels, downs, block, block)
    held = [in_hbm(env.reshape(env_shape)) for env in (left_env_a, right_env_a, left_env_b, right_env_b)]
    bits = 2 * downs * block * block
    env_bytes = channels * bits
    apply_flops = 4 * channels * downs * block**3
    sizes = in_hbm(sector_sizes.transpose(0, 2, 3, 1))
    tile = jax.ShapeDtypeStruct((8, 128), F32)

    (starts,) = call(
        masked_starts,
        "masked_starts",
        [HBM, HBM, HBM],
        [(VMEM, pltpu.VMEM(both, BF16))],
        [pltpu.SMEM(sizes.shape, jnp.int32), pltpu.SemaphoreType.DMA(()), pltpu.SemaphoreType.DMA((BONDS,))],
        4 * downs * block * block,
        4 * bits,
    )(sizes, in_hbm(guess_a.reshape(pair)), in_hbm(guess_b.reshape(pair)))
    swapped, shifted = swapped_pairs(starts), shifted_pairs(starts)

    list_shape = (LIST_ROWS, channels * downs + 1)
    sources = pltpu.VMEM((BONDS, 2 * downs, block, block), BF16)
    *loaded, images, near_rest, row, lists = call(
        opening,
        "opening",
        [HBM, VMEM, VMEM] + [HBM] * 4,
        [(VMEM, pltpu.VMEM(env_shape, BF16))] * 4
        + [
            (VMEM, pltpu.VMEM((2,) + both, F32)),
            (VMEM, pltpu.VMEM(both, F32)),
            (VMEM, tile),
            (SMEM, jax.ShapeDtypeStruct(list_shape, jnp.int32)),
        ],
        [
            sources,
            pltpu.SMEM((channels,), jnp.int32),
            pltpu.SemaphoreType.DMA(()),
            pltpu.SemaphoreType.DMA((channels,)),
        ],
        apply_flops,
        5 * env_bytes,
    )(in_hbm(term_shift), starts, swapped, *held)

    rest, sent = call(
        first_images,
        "first_images",
        [VMEM, HBM] + [VMEM] * 6,
        [
            (VMEM, pltpu.VMEM(both, F32)),
            (VMEM, pltpu.VMEM(both, BF16)),
        ],
        [
            pltpu.SMEM(list_shape, jnp.int32),
            pltpu.SMEM(sizes.shape, jnp.int32),
            pltpu.SemaphoreType.DMA((2,)),
        ],
        apply_flops,
        env_bytes,
    )(lists, sizes, *loaded, shifted, near_rest)
    swapped, shifted = swapped_pairs(sent), shifted_pairs(sent)
    row, sums, along = call(
        early_seconds,
        "early_seconds",
        [VMEM] * 11,
        [
            (VMEM, tile),
            (VMEM, pltpu.VMEM(both, F32)),
            (HBM, jax.ShapeDtypeStruct((2,) + pair, BF16)),
        ],
        [
            sources,
            pltpu.SMEM(list_shape, jnp.int32),
            pltpu.SemaphoreType.DMA(()),
            pltpu.SemaphoreType.DMA((2,)),
        ],
        apply_flops,
        env_bytes,
    )(lists, *loaded, sent, swapped, starts, rest, images, row)
    from_next = from_right_segment(along)
    (row,) = call(
        late_seconds,
        "late_seconds",
        [VMEM] * 10,
        [(VMEM, pltpu.VMEM((devices, 128), F32))],
        [
            pltpu.VMEM(both, F32),
            pltpu.SMEM(list_shape, jnp.int32),
            pltpu.SemaphoreType.DMA(()),
        ],
        apply_flops,
        env_bytes,
    )(lists, *loaded, shifted, starts, rest, sums, row)
    numbers = lax.all_to_all(row, ("seg", "blk"), 0, 0, tiled=True)
    (mixed,) = call(
        mixing,
        "mixing",
        [VMEM, VMEM, HBM],
        [(VMEM, jax.ShapeDtypeStruct(env_shape, BF16))],
        [],
        4 * channels * channels * GROUP * downs * block * block,
        2 * env_bytes,
    )(channel_mix, loaded[0], row)
    state32 = jax.ShapeDtypeStruct(pair, F32)
    ground_a, ground_b, energies, boundary = call(
        functools.partial(finish, 1.0 / block, ups),
        "finish",
        [VMEM] + [HBM] * 5,
        [
            (HBM, state32),
            (HBM, state32),
            (HBM, jax.ShapeDtypeStruct((1, 2), F32)),
            (HBM, jax.ShapeDtypeStruct(env_shape, BF16)),
        ],
        [
            pltpu.VMEM((1, 2), F32),
            pltpu.VMEM(both, BF16),
            pltpu.VMEM(both, F32),
            pltpu.VMEM((2,) + pair, BF16),
            pltpu.VMEM(pair, BF16),
            pltpu.VMEM(env_shape, BF16),
            pltpu.VMEM(env_shape, BF16),
            pltpu.VMEM(both, F32),
            pltpu.SemaphoreType.DMA((7,)),
            pltpu.SemaphoreType.DMA((channels,)),
            pltpu.SemaphoreType.DMA((channels + BONDS,)),
        ],
        apply_flops,
        2 * env_bytes,
    )(
        numbers,
        *(in_hbm(x) for x in (starts, rest, from_next, edge_state.reshape(pair), mixed)),
    )
    return (
        ground_a.reshape(guess_a.shape),
        ground_b.reshape(guess_b.shape),
        energies,
        boundary.reshape(left_env_a.shape),
    )


def solution(mesh):
    placed = (
        P("seg", "blk", None, None, None),
        P("seg", "blk", None, None, None),
        P("seg", None, "blk", None, None, None),
        P("seg", None, "blk", None, None, None),
        P("seg", None, "blk", None, None, None),
        P("seg", None, "blk", None, None, None),
        P(),
        P(),
        P("seg", None, "blk", None),
        P("blk", None, None, None),
    )
    return jax.shard_map(
        local,
        mesh=mesh,
        in_specs=placed,
        out_specs=(
            P("seg", "blk", None, None, None),
            P("seg", "blk", None, None, None),
            P("seg", None),
            P("seg", None, "blk", None, None, None),
        ),
        check_vma=False,
    )
```

```python
import functools

import jax
import jax.numpy as jnp
from jax import lax
from jax.experimental import pallas as pl
from jax.experimental.pallas import tpu as pltpu
from jax.sharding import PartitionSpec as P

F32 = jnp.float32
BF16 = jnp.bfloat16
VMEM = pl.BlockSpec(memory_space=pltpu.VMEM)
SMEM = pl.BlockSpec(memory_space=pltpu.SMEM)
HBM = pl.BlockSpec(memory_space=pltpu.HBM)
MIB = 1 << 20
GROUP = 16
BATCH = 6
BONDS = 2

CHANNEL, KIND, DOWN, SOURCE, OPENS = range(5)
EARLY, LATE = 0, OPENS + 1
LIST_ROWS = LATE + SOURCE + 1


(
    SIZE,
    QUOTIENT,
    REST,
    START_REST,
    REST_IMAGE,
    START_IMAGE,
    REST_OWN,
    REST_SWAPPED,
    START_OWN,
    START_SWAPPED,
) = range(10)
BOND_LANES = 64


def call(body, name, ins, outs, scratch, flops, moved, limit=20 * MIB):
    return pl.pallas_call(
        body,
        name=name,
        in_specs=ins,
        out_specs=tuple(spec for spec, _ in outs),
        out_shape=tuple(shape for _, shape in outs),
        scratch_shapes=scratch,
        cost_estimate=pl.CostEstimate(flops=flops, bytes_accessed=moved, transcendentals=0),
        compiler_params=pltpu.CompilerParams(vmem_limit_bytes=limit),
    )


def in_hbm(array):
    return pltpu.with_memory_space_constraint(array, pltpu.HBM)


def live(rows, cols, block):
    row = lax.broadcasted_iota(jnp.int32, (block, block), 0)
    col = lax.broadcasted_iota(jnp.int32, (block, block), 1)
    return (row < rows) & (col < cols)


def live_of(sizes, bond, down, block):
    return live(sizes[0, 0, down, 2 * bond], sizes[0, 0, down, 2 * bond + 1], block)


def dot(left, right):
    return jnp.dot(left, right, preferred_element_type=F32)


def dot_by_rows(left, right):
    return lax.dot_general(left, right, (((1,), (1,)), ((), ())), preferred_element_type=F32)


def exact_dot(left, right):
    return jnp.dot(left, right, precision=lax.Precision.HIGHEST, preferred_element_type=F32)


def total(array):
    return jnp.sum(jnp.sum(array, axis=0, keepdims=True), axis=1, keepdims=True)


def folded(array):
    return jnp.sum(array.reshape(-1, 8, array.shape[-1]), axis=0)


def totals(parts):
    rows = parts[0].shape[0]
    by_row = jnp.sum(jnp.concatenate(parts), axis=1, keepdims=True)
    return [
        jnp.sum(by_row[i * rows : (i + 1) * rows], axis=0, keepdims=True) for i in range(len(parts))
    ]


def in_lanes(width, pairs):
    lane = lax.broadcasted_iota(jnp.int32, (1, width), 1)
    row = jnp.zeros((1, width), F32)
    for place, value in pairs:
        row = jnp.where(lane == place, value, row)
    return row


def masked_starts(sizes_held, guess_a, guess_b, starts, sizes, size_sem, sems):
    sizes_copy = pltpu.make_async_copy(sizes_held, sizes, size_sem)
    sizes_copy.start()
    downs, block = starts.shape[1], starts.shape[-1]
    copies = [
        pltpu.make_async_copy(guess, starts.at[bond], sems.at[bond])
        for bond, guess in enumerate((guess_a, guess_b))
    ]
    for copy in copies:
        copy.start()
    sizes_copy.wait()
    for bond, down in [(bond, down) for bond in range(BONDS) for down in range(downs)]:
        if down == 0:
            copies[bond].wait()
        start = starts[bond, down]
        starts[bond, down] = jnp.where(
            live_of(sizes, bond, down, block), start, jnp.zeros_like(start)
        )


def is_late(code):
    even = lax.rem(lax.axis_index("blk"), 2) == 0
    return code == jnp.where(even, 1, 2)


def list_units(shift, downs, lists):
    channels = shift.shape[0]
    end = channels * downs
    early, late = jnp.int32(0), jnp.int32(0)
    for channel in range(channels):
        code = shift[channel]
        far = is_late(code)
        near = jnp.logical_not(far) & ((code == 1) | (code == 2))
        move = (code == 4).astype(jnp.int32) - (code == 3).astype(jnp.int32)
        opens = jnp.int32(1)
        for down in range(downs):
            source = down + move
            here = jnp.logical_not(far) & (source >= 0) & (source < downs)
            lists[EARLY + CHANNEL, early] = jnp.int32(channel)
            lists[EARLY + KIND, early] = near.astype(jnp.int32)
            lists[EARLY + DOWN, early] = jnp.int32(down)
            lists[EARLY + SOURCE, early] = jnp.where(near, downs + down, source)
            lists[EARLY + OPENS, early] = opens
            lists[LATE + CHANNEL, late] = jnp.int32(channel)
            lists[LATE + KIND, late] = jnp.int32(0)
            lists[LATE + DOWN, late] = jnp.int32(down)
            lists[LATE + SOURCE, late] = jnp.int32(down)
            opens = jnp.where(here, 0, opens)
            early = early + here.astype(jnp.int32)
            late = late + far.astype(jnp.int32)
    lists[EARLY, end] = early
    lists[LATE, end] = late


class Unparted:
    def __init__(self, sums):
        self.sums = sums

    def __getitem__(self, place):
        return self.sums[place[1:]]

    def __setitem__(self, place, value):
        self.sums[place[1:]] = value


def add_units(lists, base, lefts, rights, sources, sums, arrived=None):
    def images(indices):
        units = [
            [lists[base + part, index] for part in (CHANNEL, KIND, DOWN, SOURCE)]
            for index in indices
        ]
        if arrived is not None:
            for index, unit in zip(indices, units):
                pl.when(lists[base + OPENS, index] == 1)(functools.partial(arrived, unit[0]))
        halves = [
            [
                dot(lefts[bond][channel, down], sources[bond, source]).astype(BF16)
                for bond in range(BONDS)
            ]
            for channel, _, down, source in units
        ]
        for (channel, kind, down, _), half in zip(units, halves):
            for bond in range(BONDS):
                sums[kind, bond, down] += dot_by_rows(half[bond], rights[bond][channel, down])

    count = lists[base, lists.shape[1] - 1]
    done = jnp.int32(0)
    for size in (4, 2, 1):
        steps = lax.div(count - done, size)

        def step(index, carry, size=size, done=done):
            first = done + size * index
            images([first + i for i in range(size)])
            return carry

        lax.fori_loop(0, steps, step, 0)
        done = done + size * steps


def fill_sources(own, swapped, sources):
    downs = own.shape[1]
    for bond in range(BONDS):
        for down in range(downs):
            sources[bond, down] = own[bond, down]
            sources[bond, downs + down] = swapped[bond, down]


def opening(shift_held, starts, swapped, *refs):
    held, loaded, (images, near_rest, row, lists, sources, shift, shift_sem, sems) = (
        refs[:4],
        refs[4:8],
        refs[8:],
    )
    shift_copy = pltpu.make_async_copy(shift_held, shift, shift_sem)
    shift_copy.start()
    left_a, right_a, left_b, right_b = loaded
    channels, downs = left_a.shape[0], left_a.shape[1]

    def copies(channel):
        return [
            pltpu.make_async_copy(source.at[channel], target.at[channel], sems.at[channel])
            for source, target in zip(held, loaded)
        ]

    def await_one(channel):
        for copy in copies(channel):
            copy.wait()

    for channel in range(channels):
        for copy in copies(channel):
            copy.start()
    shift_copy.wait()
    list_units(shift, downs, lists)
    images[...] = jnp.zeros_like(images)
    fill_sources(starts, swapped, sources)
    found = []
    for bond in range(BONDS):
        size = jnp.zeros((1, 1), F32)
        for down in range(downs):
            start = starts[bond, down].astype(F32)
            size += total(start * start)
        found.append((bond * BOND_LANES + SIZE, size))
    add_units(lists, EARLY, (left_a, left_b), (right_a, right_b), sources, images, await_one)
    pairs = [(bond, kind) for bond in range(BONDS) for kind in range(2)]
    crosses = totals(
        [
            sum(
                folded(starts[bond, down].astype(F32) * images[kind, bond, down])
                for down in range(downs)
            )
            for bond, kind in pairs
        ]
    )
    for (bond, kind), cross in zip(pairs, crosses):
        found.append((bond * BOND_LANES + START_OWN + kind, cross))
    for bond in range(BONDS):
        size = found[bond][1]
        cross = crosses[2 * bond] + crosses[2 * bond + 1]
        quotient = jnp.where(size > 0.0, cross / jnp.where(size > 0.0, size, 1.0), 0.0)
        found.append((bond * BOND_LANES + QUOTIENT, quotient))
        for down in range(downs):
            image = images[0, bond, down] + images[1, bond, down]
            near_rest[bond, down] = image - quotient * starts[bond, down].astype(F32)
    row[...] = jnp.broadcast_to(in_lanes(row.shape[1], found), row.shape)
    for channel in range(channels):
        pl.when(is_late(shift[channel]))(functools.partial(await_one, channel))


def mixing(mix, env, after, mixed):
    del after
    channels, downs, block = env.shape[0], env.shape[1], env.shape[-1]
    wide = channels * GROUP
    squared = exact_dot(mix[...], mix[...])
    spread_rows = (
        lax.broadcasted_iota(jnp.int32, (wide, channels), 0) // GROUP
        == lax.broadcasted_iota(jnp.int32, (wide, channels), 1)
    ).astype(F32)
    spread_cols = (
        lax.broadcasted_iota(jnp.int32, (channels, wide), 1) // GROUP
        == lax.broadcasted_iota(jnp.int32, (channels, wide), 0)
    ).astype(F32)
    spread = exact_dot(exact_dot(spread_rows, squared), spread_cols)
    same = lax.rem(lax.broadcasted_iota(jnp.int32, (wide, wide), 0), GROUP) == lax.rem(
        lax.broadcasted_iota(jnp.int32, (wide, wide), 1), GROUP
    )
    spread = jnp.where(same, spread, 0.0)
    mix_high = spread.astype(BF16)
    mix_low = (spread - mix_high.astype(F32)).astype(BF16)
    for down in range(downs):
        for group in range(block // GROUP):
            rows = slice(group * GROUP, (group + 1) * GROUP)
            part = env[:, down, rows, :].reshape(wide, block)
            made = dot(mix_high, part) + dot(mix_low, part)
            mixed[:, down, rows, :] = made.astype(BF16).reshape(channels, GROUP, block)


def first_images(
    lists_held,
    sizes_held,
    left_a,
    right_a,
    left_b,
    right_b,
    shifted,
    near_rest,
    rest,
    sent,
    lists,
    sizes,
    sems,
):
    lists_copy = pltpu.make_async_copy(lists_held, lists, sems.at[0])
    lists_copy.start()
    sizes_copy = pltpu.make_async_copy(sizes_held, sizes, sems.at[1])
    sizes_copy.start()
    downs, block = left_a.shape[1], left_a.shape[-1]
    rest[...] = near_rest[...]
    lists_copy.wait()
    add_units(lists, LATE, (left_a, left_b), (right_a, right_b), shifted, Unparted(rest))
    sizes_copy.wait()
    for bond in range(BONDS):
        for down in range(downs):
            left_over = jnp.where(live_of(sizes, bond, down, block), rest[bond, down], 0.0)
            rest[bond, down] = left_over
            sent[bond, down] = left_over.astype(BF16)


def early_seconds(
    lists_held,
    left_a,
    right_a,
    left_b,
    right_b,
    sent,
    swapped,
    starts,
    rest,
    images,
    row_in,
    row,
    sums,
    along,
    sources,
    lists,
    lists_sem,
    sems,
):
    lists_copy = pltpu.make_async_copy(lists_held, lists, lists_sem)
    lists_copy.start()
    downs = left_a.shape[1]
    copies = [
        pltpu.make_async_copy(source.at[BONDS - 1], along.at[index], sems.at[index])
        for index, source in enumerate((starts, sent))
    ]
    for copy in copies:
        copy.start()
    sums[...] = jnp.zeros_like(sums)
    fill_sources(sent, swapped, sources)
    lists_copy.wait()
    add_units(lists, EARLY, (left_a, left_b), (right_a, right_b), sources, Unparted(sums))
    places, parts = [], []
    for bond in range(BONDS):
        folds = {place: 0.0 for place in (REST, START_REST, REST_OWN, REST_SWAPPED)}
        for down in range(downs):
            left_over = rest[bond, down]
            folds[START_REST] += folded(left_over * starts[bond, down].astype(F32))
            folds[REST] += folded(left_over * left_over)
            for kind in range(2):
                folds[REST_OWN + kind] += folded(left_over * images[kind, bond, down])
        places += [bond * BOND_LANES + place for place in folds]
        parts += folds.values()
    found = list(zip(places, totals(parts)))
    row[...] = row_in[...] + jnp.broadcast_to(in_lanes(row.shape[1], found), row.shape)
    for copy in copies:
        copy.wait()


def late_seconds(
    lists_held,
    left_a,
    right_a,
    left_b,
    right_b,
    shifted,
    starts,
    rest,
    early_sums,
    row_in,
    row,
    lists,
    lists_sem,
):
    lists_copy = pltpu.make_async_copy(lists_held, lists, lists_sem)
    lists_copy.start()
    lefts, rights = (left_a, left_b), (right_a, right_b)
    downs = left_a.shape[1]
    places = [
        bond * BOND_LANES + place for bond in range(BONDS) for place in (REST_IMAGE, START_IMAGE)
    ]

    def with_image(parts, bond, down, image):
        parts[2 * bond] += folded(rest[bond, down] * image)
        parts[2 * bond + 1] += folded(starts[bond, down].astype(F32) * image)

    def with_units(indices, parts):
        parts = list(parts)
        units = [
            [lists[LATE + part, index] for part in (CHANNEL, DOWN, SOURCE)] for index in indices
        ]
        halves = [
            [
                dot(lefts[bond][channel, down], shifted[bond, source]).astype(BF16)
                for bond in range(BONDS)
            ]
            for channel, down, source in units
        ]
        for (channel, down, _), half in zip(units, halves):
            for bond in range(BONDS):
                image = dot_by_rows(half[bond], rights[bond][channel, down])
                with_image(parts, bond, down, image)
        return tuple(parts)

    parts = [jnp.zeros((8, rest.shape[-1]), F32) for _ in places]
    for bond in range(BONDS):
        for down in range(downs):
            with_image(parts, bond, down, early_sums[bond, down])
    parts = tuple(parts)
    lists_copy.wait()
    count = lists[LATE, lists.shape[1] - 1]
    done = jnp.int32(0)
    for size in (4, 2, 1):
        steps = lax.div(count - done, size)

        def step(index, parts, size=size, done=done):
            first = done + size * index
            return with_units([first + i for i in range(size)], parts)

        parts = lax.fori_loop(0, steps, step, parts)
        done = done + size * steps
    found = list(zip(places, totals(list(parts))))
    row[...] = jnp.broadcast_to(row_in[0:1, :] + in_lanes(row.shape[1], found), row.shape)


def ritz(numbers, bond, first, ups, place):
    lane = lax.broadcasted_iota(jnp.int32, (1, numbers.shape[1]), 1)
    inside = (lane >= first) & (lane < first + ups)

    def part(index):
        at = bond * BOND_LANES + index
        return numbers[at : at + 1]

    def over_ups(values):
        return jnp.sum(jnp.where(inside, values, 0.0), axis=1, keepdims=True)

    size = part(SIZE)
    quotient = part(QUOTIENT)
    rest_sq = part(REST)
    start_rest = part(START_REST)
    low = pltpu.roll(quotient, 1, 1)
    high = pltpu.roll(quotient, quotient.shape[1] - 1, 1)
    even = (lane & 1) == 0
    none_low, none_high = lane == first, lane == first + ups - 1
    norm_sq = over_ups(size)
    alpha_zero = over_ups(size * quotient + start_rest) / norm_sq
    off = quotient - alpha_zero
    off_low = jnp.where(none_low, 0.0, low - alpha_zero)
    off_high = jnp.where(none_high, 0.0, high - alpha_zero)
    off_swapped = jnp.where(even, off_high, off_low)
    off_shifted = jnp.where(even, off_low, off_high)
    along_start = jnp.where(size > 0.0, start_rest / jnp.where(size > 0.0, size, 1.0), 0.0)
    across_sq = jnp.maximum(rest_sq - start_rest * along_start, 0.0)
    residual_sq = over_ups(across_sq + size * (off + along_start) * (off + along_start))
    crossed = part(REST_IMAGE) + off * part(START_IMAGE)
    rest_of = [part(REST_OWN), part(REST_SWAPPED)]
    start_of = [part(START_OWN), part(START_SWAPPED)]
    rest_of.append(rest_sq + quotient * start_rest - rest_of[0] - rest_of[1])
    start_of.append(start_rest + quotient * size - start_of[0] - start_of[1])
    for factor, of_rest, of_start in zip((off, off_swapped, off_shifted), rest_of, start_of):
        crossed += factor * (of_rest + off * of_start)
    alpha_one = over_ups(crossed) / residual_sq
    beta_sq = residual_sq / norm_sq
    beta = jnp.sqrt(beta_sq)
    spread = 0.5 * (alpha_zero - alpha_one)
    energy = 0.5 * (alpha_zero + alpha_one) - jnp.sqrt(spread * spread + beta_sq)
    weight_one = energy - alpha_zero
    length = jnp.sqrt(beta_sq + weight_one * weight_one)
    of_rest = weight_one / (beta * length)
    own_off = jnp.sum(jnp.where(lane == first + place, off, 0.0), axis=1, keepdims=True)
    return energy, beta / length + of_rest * own_off, of_rest


def finish(
    factor,
    ups,
    numbers,
    starts_held,
    rest_held,
    along_held,
    edge_held,
    mixed_held,
    ground_a,
    ground_b,
    energies_out,
    boundary,
    energies,
    starts,
    rest,
    along,
    edge,
    mixed,
    made,
    grounds,
    in_sems,
    mixed_sems,
    out_sems,
):
    channels, downs = mixed.shape[0], mixed.shape[1]

    def arrival(index, source, target):
        copy = pltpu.make_async_copy(source, target, in_sems.at[index])
        copy.start()
        return copy

    first = [
        arrival(0, starts_held.at[0], starts.at[0]),
        arrival(1, rest_held.at[0], rest.at[0]),
        arrival(2, along_held, along),
        arrival(3, edge_held, edge),
    ]
    groups = []
    while sum(map(len, groups)) < channels:
        at = sum(map(len, groups))
        groups.append(range(at, at + min(BATCH, (channels - at + 1) // 2)))

    def part(array, group):
        return array.at[group.start : group.stop]

    arrivals = [
        pltpu.make_async_copy(part(mixed_held, group), part(mixed, group), mixed_sems.at[index])
        for index, group in enumerate(groups)
    ]
    arrivals[0].start()
    second = [arrival(4, starts_held.at[1], starts.at[1]), arrival(5, rest_held.at[1], rest.at[1])]
    for copy in arrivals[1:]:
        copy.start()
    devices, width = numbers.shape
    segments = devices // ups
    seg, blk = lax.axis_index("seg"), lax.axis_index("blk")
    after = jnp.minimum(seg + 1, segments - 1)
    padding = [jnp.zeros((-devices % width, width), F32)] if devices % width else []
    by_place = jnp.concatenate([numbers[...], *padding]).T
    solves = [
        ritz(by_place, bond, at * ups, ups, blk) for bond, at in ((0, seg), (1, seg), (1, after))
    ]
    energy, of_start, of_rest = zip(*solves)
    lane = lax.broadcasted_iota(jnp.int32, energies.shape, 1)
    energies[...] = jnp.where(lane == 0, energy[0], energy[1])
    last = seg == segments - 1
    out_copies = [pltpu.make_async_copy(energies, energies_out, in_sems.at[6])]
    out_copies[0].start()

    def leave(index, source, target):
        copy = pltpu.make_async_copy(source, target, out_sems.at[index])
        copy.start()
        out_copies.append(copy)

    def ground_of(bond, target):
        for down in range(downs):
            start = starts[bond, down].astype(F32)
            grounds[bond, down] = of_start[bond] * start + of_rest[bond] * rest[bond, down]
        leave(channels + bond, grounds.at[bond], target)

    for copy in first:
        copy.wait()
    products = []
    for down in range(downs):
        start = starts[0, down].astype(F32)
        ground = of_start[0] * start + of_rest[0] * rest[0, down]
        grounds[0, down] = ground
        found = of_start[2] * along[0, down].astype(F32) + of_rest[2] * along[1, down].astype(F32)
        state = jnp.where(last, edge[down], found.astype(BF16))
        product = (dot(ground.astype(BF16), state) * factor).astype(BF16)
        products.append((product, product.T))
    leave(channels, grounds.at[0], ground_a)
    halves = {}

    def last_product(index):
        for channel in groups[index]:
            for down, (_, turned) in enumerate(products):
                made[channel, down] = dot(turned, halves[channel, down]).astype(BF16)
        leave(index, part(made, groups[index]), part(boundary, groups[index]))

    for index, group in enumerate(groups):
        arrivals[index].wait()
        for down, (product, _) in enumerate(products):
            block = product.shape[0]
            stacked = mixed[group.start : group.stop, down].reshape(len(group) * block, block)
            half = dot(stacked, product).astype(BF16)
            for place, channel in enumerate(group):
                halves[channel, down] = half[place * block : (place + 1) * block]
        if index > 0:
            last_product(index - 1)
        if index == 0:
            for copy in second:
                copy.wait()
            ground_of(1, ground_b)
    last_product(len(groups) - 1)
    for copy in out_copies:
        copy.wait()


def swapped_pairs(block):
    devices = range(lax.axis_size("blk"))
    return lax.ppermute(block, "blk", [(i, i ^ 1) for i in devices if i ^ 1 in devices])


def shifted_pairs(block):
    devices = range(lax.axis_size("blk"))
    pairs = [(i, i + 1) for i in devices if i % 2 == 1 and i + 1 in devices]
    return lax.ppermute(block, "blk", pairs + [(j, i) for i, j in pairs])


def from_right_segment(block):
    segments = lax.axis_size("seg")
    return lax.ppermute(block, "seg", [(i + 1, i) for i in range(segments - 1)])


def local(
    guess_a,
    guess_b,
    left_env_a,
    right_env_a,
    left_env_b,
    right_env_b,
    channel_mix,
    term_shift,
    sector_sizes,
    edge_state,
):
    block = guess_a.shape[-1]
    downs = guess_a.shape[2]
    channels = left_env_a.shape[1]
    ups = lax.axis_size("blk")
    devices = ups * lax.axis_size("seg")
    pair = (downs, block, block)
    both = (BONDS,) + pair
    env_shape = (channels, downs, block, block)
    held = [in_hbm(env.reshape(env_shape)) for env in (left_env_a, right_env_a, left_env_b, right_env_b)]
    bits = 2 * downs * block * block
    env_bytes = channels * bits
    apply_flops = 4 * channels * downs * block**3
    sizes = in_hbm(sector_sizes.transpose(0, 2, 3, 1))
    tile = jax.ShapeDtypeStruct((8, 128), F32)

    (starts,) = call(
        masked_starts,
        "masked_starts",
        [HBM, HBM, HBM],
        [(VMEM, pltpu.VMEM(both, BF16))],
        [pltpu.SMEM(sizes.shape, jnp.int32), pltpu.SemaphoreType.DMA(()), pltpu.SemaphoreType.DMA((BONDS,))],
        4 * downs * block * block,
        4 * bits,
    )(sizes, in_hbm(guess_a.reshape(pair)), in_hbm(guess_b.reshape(pair)))
    swapped, shifted = swapped_pairs(starts), shifted_pairs(starts)

    list_shape = (LIST_ROWS, channels * downs + 1)
    sources = pltpu.VMEM((BONDS, 2 * downs, block, block), BF16)
    *loaded, images, near_rest, row, lists = call(
        opening,
        "opening",
        [HBM, VMEM, VMEM] + [HBM] * 4,
        [(VMEM, pltpu.VMEM(env_shape, BF16))] * 4
        + [
            (VMEM, pltpu.VMEM((2,) + both, F32)),
            (VMEM, pltpu.VMEM(both, F32)),
            (VMEM, tile),
            (SMEM, jax.ShapeDtypeStruct(list_shape, jnp.int32)),
        ],
        [
            sources,
            pltpu.SMEM((channels,), jnp.int32),
            pltpu.SemaphoreType.DMA(()),
            pltpu.SemaphoreType.DMA((channels,)),
        ],
        apply_flops,
        5 * env_bytes,
    )(in_hbm(term_shift), starts, swapped, *held)

    rest, sent = call(
        first_images,
        "first_images",
        [VMEM, HBM] + [VMEM] * 6,
        [
            (VMEM, pltpu.VMEM(both, F32)),
            (VMEM, pltpu.VMEM(both, BF16)),
        ],
        [
            pltpu.SMEM(list_shape, jnp.int32),
            pltpu.SMEM(sizes.shape, jnp.int32),
            pltpu.SemaphoreType.DMA((2,)),
        ],
        apply_flops,
        env_bytes,
    )(lists, sizes, *loaded, shifted, near_rest)
    swapped, shifted = swapped_pairs(sent), shifted_pairs(sent)
    row, sums, along = call(
        early_seconds,
        "early_seconds",
        [VMEM] * 11,
        [
            (VMEM, tile),
            (VMEM, pltpu.VMEM(both, F32)),
            (HBM, jax.ShapeDtypeStruct((2,) + pair, BF16)),
        ],
        [
            sources,
            pltpu.SMEM(list_shape, jnp.int32),
            pltpu.SemaphoreType.DMA(()),
            pltpu.SemaphoreType.DMA((2,)),
        ],
        apply_flops,
        env_bytes,
    )(lists, *loaded, sent, swapped, starts, rest, images, row)
    from_next = from_right_segment(along)
    (row,) = call(
        late_seconds,
        "late_seconds",
        [VMEM] * 10,
        [(VMEM, pltpu.VMEM((devices, 128), F32))],
        [pltpu.SMEM(list_shape, jnp.int32), pltpu.SemaphoreType.DMA(())],
        apply_flops,
        env_bytes,
    )(lists, *loaded, shifted, starts, rest, sums, row)
    numbers = lax.all_to_all(row, ("seg", "blk"), 0, 0, tiled=True)
    (mixed,) = call(
        mixing,
        "mixing",
        [VMEM, VMEM, HBM],
        [(VMEM, jax.ShapeDtypeStruct(env_shape, BF16))],
        [],
        4 * channels * channels * GROUP * downs * block * block,
        2 * env_bytes,
    )(channel_mix, loaded[0], row)
    state32 = jax.ShapeDtypeStruct(pair, F32)
    ground_a, ground_b, energies, boundary = call(
        functools.partial(finish, 1.0 / block, ups),
        "finish",
        [VMEM] + [HBM] * 5,
        [
            (HBM, state32),
            (HBM, state32),
            (HBM, jax.ShapeDtypeStruct((1, 2), F32)),
            (HBM, jax.ShapeDtypeStruct(env_shape, BF16)),
        ],
        [
            pltpu.VMEM((1, 2), F32),
            pltpu.VMEM(both, BF16),
            pltpu.VMEM(both, F32),
            pltpu.VMEM((2,) + pair, BF16),
            pltpu.VMEM(pair, BF16),
            pltpu.VMEM(env_shape, BF16),
            pltpu.VMEM(env_shape, BF16),
            pltpu.VMEM(both, F32),
            pltpu.SemaphoreType.DMA((7,)),
            pltpu.SemaphoreType.DMA((channels,)),
            pltpu.SemaphoreType.DMA((channels + BONDS,)),
        ],
        apply_flops,
        2 * env_bytes,
    )(
        numbers,
        *(in_hbm(x) for x in (starts, rest, from_next, edge_state.reshape(pair), mixed)),
    )
    return (
        ground_a.reshape(guess_a.shape),
        ground_b.reshape(guess_b.shape),
        energies,
        boundary.reshape(left_env_a.shape),
    )


def solution(mesh):
    placed = (
        P("seg", "blk", None, None, None),
        P("seg", "blk", None, None, None),
        P("seg", None, "blk", None, None, None),
        P("seg", None, "blk", None, None, None),
        P("seg", None, "blk", None, None, None),
        P("seg", None, "blk", None, None, None),
        P(),
        P(),
        P("seg", None, "blk", None),
        P("blk", None, None, None),
    )
    return jax.shard_map(
        local,
        mesh=mesh,
        in_specs=placed,
        out_specs=(
            P("seg", "blk", None, None, None),
            P("seg", "blk", None, None, None),
            P("seg", None),
            P("seg", None, "blk", None, None, None),
        ),
        check_vma=False,
    )
```
